512 devices in a mesh: tx: 8 (over x, core), rx: 16 (over z), freq: 4 (over y).
Axes of the slice: x: 4, y: 4, z: 16, core: 2. Of those that a mesh axis runs over, the one named last changes fastest.
Arguments:
- spectrum: float32 [2, 8, 2048, 2048], P(None, 'freq', 'tx', 'rx'), may hold values from -6 to 6
- measured: float32 [2, 8, 2048, 2048], P(None, 'freq', 'tx', 'rx'), may hold values from -12 to 12
- wavenumber: float32 [8], replicated, may hold values from 1.5 to 3
- send_weight: float32 [2048], P('tx'), may hold values from 0.25 to 2
- hear_weight: float32 [2048], P('rx'), may hold values from 0.25 to 2
- aperture: int32 [128, 128], P('tx', 'rx'), may hold values 0 or 1
Outputs:
- updated: float32 [2, 8, 2048, 2048], P(None, 'freq', 'tx', 'rx')
- residual: float32 [2, 8, 2048, 2048], P(None, 'freq', 'tx', 'rx')
The draws below stay inside these ranges and needn't reach their ends.
Inputs may be any that keep to these rules, and one draw needn't show every extreme that they name: `aperture`: 1 marks a live tile of 16 x 16 antenna pairs, 0 a silent one.
All inputs are finite; a program needn't handle non-finite values. No bound on the sum of `aperture` on one device may be relied on, other than what follows from the above.
Results may differ from the reference program's by a relative error of at most 0.00016.
Values sent between devices are 32-bit elements; how exact they have to be, the bound alone decides.
No kernel may reach another device: no remote copies, remote signals or barrier semaphores. Data moves between devices by JAX's collectives and lax.ppermute only.
A program may use at most 128 MiB of HBM per device.

```python
import math
import jax
import jax.numpy as jnp
from jax import lax

F = 8
NT = 2048
NR = 2048
TILE = 16
DEPTH = 8


def with_ends(values, rng, least, top_value):
    shape = values.shape
    spot = [jax.random.randint(jax.random.fold_in(rng, axis), (), 0, shape[axis]) for axis in range(len(shape))]
    values = values.at[tuple(spot)].set(least)
    longest = shape.index(max(shape))
    spot[longest] = (spot[longest] + 1) % shape[longest]
    return values.at[tuple(spot)].set(top_value)


def level_of(stream_key, extent, split, smallest, largest):
    factor_of, own = 1.0, jax.random.fold_in(stream_key, 6)
    for position, blocks in split:
        steps = jnp.exp(jax.random.uniform(jax.random.fold_in(own, position), (blocks,), jnp.float32, smallest / len(split), largest / len(split)))
        factor_of = factor_of * jnp.repeat(steps, extent[position] // blocks).reshape([-1 if axis == position else 1 for axis in range(len(extent))])
    return factor_of


def noise(key, shape, deviation, reach, pieces=(), kind=jnp.bfloat16):
    values = deviation * jax.random.normal(key, shape, jnp.float32)
    if pieces:
        values = values * level_of(key, shape, pieces, -0.22, 0.18)
    return jnp.clip(values, -reach, reach).astype(kind)


def setup_inputs(seed: int = 0) -> dict:
    streams_of = jax.random.split(jax.random.key(seed), 7)
    spectrum = noise(streams_of[0], (2, DEPTH, NT, NR), 1.0, 6.0, ((1, 4), (2, 8), (3, 16)), jnp.float32)
    measured = noise(streams_of[1], (2, F, NT, NR), 2.0, 12.0, ((1, 4), (2, 8), (3, 16)), jnp.float32)
    wavenumber = jnp.clip(jax.random.uniform(streams_of[2], (F,), jnp.float32, 1.5, 3.0), 1.5, 3.0)
    send_weight = jnp.clip(jnp.exp(math.log(2.0) - 2.0794415 * jax.random.uniform(streams_of[3], (NT,), jnp.float32) ** level_of(streams_of[3], (NT,), ((0, 8),), -0.2, 0.2)), 0.25, 2.0)
    hear_weight = jnp.clip(jnp.exp(math.log(2.0) - 2.0794415 * jax.random.uniform(streams_of[4], (NR,), jnp.float32) ** level_of(streams_of[4], (NR,), ((0, 16),), -0.2, 0.2)), 0.25, 2.0)
    aperture = with_ends((jax.random.randint(streams_of[5], (NT // TILE, NR // TILE), 0, 3) < 2).astype(jnp.int32), jax.random.fold_in(streams_of[5], 1), 0, 1)
    return dict(spectrum=spectrum, measured=measured, wavenumber=wavenumber, send_weight=send_weight, hear_weight=hear_weight, aperture=aperture)


depth_step = 2.0
step_size = 0.125
root_floor = 0.25

def wave_numbers(offset, length, total):
    indices = offset + jnp.arange(length, dtype=jnp.int32)
    signed = jnp.where(indices < total // 2, indices, indices - total)
    return 2.0 * jnp.pi / total * signed.astype(jnp.float32)

def vertical(wavenumber, waves_sent, waves_heard):
    squared = (wavenumber * wavenumber)[:, None, None]
    first_root = jnp.sqrt(jnp.maximum(squared - (waves_sent * waves_sent)[None, :, None], 0.0) + root_floor)
    second_root = jnp.sqrt(jnp.maximum(squared - (waves_heard * waves_heard)[None, None, :], 0.0) + root_floor)
    return first_root + second_root

def reference(spectrum, measured, wavenumber, send_weight, hear_weight, aperture):
    waves_sent = wave_numbers(0, NT, NT)
    waves_heard = wave_numbers(0, NR, NR)
    vertical_waves = vertical(wavenumber, waves_sent, waves_heard)
    pair_real = jnp.zeros((F, NT, NR), jnp.float32)
    pair_imag = jnp.zeros((F, NT, NR), jnp.float32)
    for depth_index in range(DEPTH):
        phases = vertical_waves * (depth_step * (depth_index + 1))
        cosine = jnp.cos(phases)
        sine_part = jnp.sin(phases)
        layer_real = spectrum[0, depth_index][None]
        layer_imag = spectrum[1, depth_index][None]
        pair_real = pair_real + (cosine * layer_real + sine_part * layer_imag)
        pair_imag = pair_imag + (cosine * layer_imag - sine_part * layer_real)
    field = jnp.fft.ifft2(lax.complex(pair_real, pair_imag), norm='ortho')
    tile_gate = jnp.repeat(jnp.repeat(aperture, TILE, axis=0), TILE, axis=1).astype(jnp.float32)
    weights = send_weight[:, None] * hear_weight[None, :] * tile_gate
    resid_real = weights[None] * (measured[0] - jnp.real(field))
    resid_imag = weights[None] * (measured[1] - jnp.imag(field))
    back = jnp.fft.fft2(lax.complex(resid_real, resid_imag), norm='ortho')
    back_real = jnp.real(back)
    back_imag = jnp.imag(back)
    layers_real = []
    layers_imag = []
    for depth_index in range(DEPTH):
        phases = vertical_waves * (depth_step * (depth_index + 1))
        cosine = jnp.cos(phases)
        sine_part = jnp.sin(phases)
        layers_real.append(lax.optimization_barrier(jnp.sum(cosine * back_real - sine_part * back_imag, axis=0)))
        layers_imag.append(lax.optimization_barrier(jnp.sum(cosine * back_imag + sine_part * back_real, axis=0)))
    gradient = jnp.stack([jnp.stack(layers_real), jnp.stack(layers_imag)])
    return (spectrum + step_size * gradient, jnp.stack([resid_real, resid_imag]))
```

```python
import functools
import math

import jax
import jax.numpy as jnp
import ml_dtypes
import numpy as np
from jax import lax
from jax.experimental import pallas as pl
from jax.experimental.pallas import tpu as pltpu
from jax.sharding import PartitionSpec as P

depth_step = 2.0
step_size = 0.125
root_floor = 0.25
bf16 = jnp.bfloat16
f32 = jnp.float32
nt_form = (((1,), (1,)), ((), ()))
params = pltpu.CompilerParams(vmem_limit_bytes=56 * 1024 * 1024)


def halves(table):
    high = table.astype(np.float32).astype(ml_dtypes.bfloat16)
    low = (table - high.astype(np.float64)).astype(np.float32).astype(ml_dtypes.bfloat16)
    return high, low


def angles(left, right, total):
    return 2.0 * np.pi / total * ((left[:, None] * right[None, :]) % total)


@functools.cache
def tables():
    index = np.arange(128)
    theta = angles(index, index, 128)
    scale = 1.0 / math.sqrt(2048.0)
    cosine, sine = np.cos(theta) * scale, np.sin(theta) * scale
    lanes = np.block([[cosine, -sine], [sine, cosine]])
    theta = angles(np.arange(16), index, 2048)
    twist_heard = np.stack([np.cos(theta), np.sin(theta)])
    twist_heard = np.broadcast_to(twist_heard[:, :, None, :], (2, 16, 8, 128)).astype(np.float32)
    z, tx, y = np.meshgrid(np.arange(16), np.arange(8), np.arange(4), indexing="ij")
    high = (tx * 64 + z * 4 + y).reshape(-1)
    theta = angles(np.arange(512), high, 512)
    cosine, sine = np.cos(theta) * scale, np.sin(theta) * scale
    long = np.zeros((2, 512, 512, 2))
    long[0, :, :, 0], long[0, :, :, 1] = cosine, -sine
    long[1, :, :, 0], long[1, :, :, 1] = sine, cosine
    long = long.reshape(1024, 1024)
    low_of_lane = np.arange(128) % 4
    theta = angles(np.arange(512), low_of_lane, 2048)
    twist_sent = np.stack([np.cos(theta), np.sin(theta)]).astype(np.float32)
    mix = np.zeros((2, 16, 2, 4, 2, 4, 2, 16))
    quarter = ((1, 0), (0, 1), (-1, 0), (0, -1))
    for r0 in range(16):
        for f0 in range(2):
            for mi in range(4):
                for t1 in range(4):
                    c, s = quarter[mi * t1 % 4]
                    mix[0, r0, f0, mi, 0, t1, f0, r0] = c
                    mix[1, r0, f0, mi, 0, t1, f0, r0] = -s
                    mix[0, r0, f0, mi, 1, t1, f0, r0] = s
                    mix[1, r0, f0, mi, 1, t1, f0, r0] = c
    mix = mix.reshape(256, 256).astype(ml_dtypes.bfloat16)
    return dict(
        lanes=halves(lanes),
        twist_heard=twist_heard,
        long=halves(long),
        long_back=halves(long.T.copy()),
        twist_sent=twist_sent,
        mix=mix,
        mix_back=mix.T.copy(),
    )


def split(value):
    high = value.astype(bf16)
    return high, (value - high.astype(f32)).astype(bf16)


def dot(left, right):
    return jnp.dot(left, right, preferred_element_type=f32)


def swap_groups(arrays, width):
    arrays = list(arrays)
    group = lax.broadcasted_iota(jnp.int32, arrays[0].shape, 1) // width
    bit = 1
    while bit < len(arrays):
        high = (group & bit) != 0
        for i in range(len(arrays)):
            if i & bit:
                continue
            a, b = arrays[i], arrays[i | bit]
            arrays[i] = jnp.where(high, pltpu.roll(b, bit * width, 1), a)
            arrays[i | bit] = jnp.where(high, b, pltpu.roll(a, 128 - bit * width, 1))
        bit *= 2
    return arrays


def times(value, c, s):
    re, im = value
    if (c, s) == (1, 0):
        return value
    if (c, s) == (0, 1):
        return -im, re
    if (c, s) == (0, -1):
        return im, -re
    if (c, s) == (-1, 0):
        return -re, -im
    return re * c - im * s, re * s + im * c


def sixteen(values, sign):
    count = len(values)
    if count == 1:
        return values
    even = sixteen(values[0::2], sign)
    odd = sixteen(values[1::2], sign)
    first, second = [], []
    for k in range(count // 2):
        if 4 * k == 0:
            turn = (1, 0)
        elif 4 * k == count:
            turn = (0, sign)
        else:
            angle = 2.0 * math.pi * k / count
            turn = (math.cos(angle), sign * math.sin(angle))
        a, b = even[k], times(odd[k], *turn)
        first.append((a[0] + b[0], a[1] + b[1]))
        second.append((a[0] - b[0], a[1] - b[1]))
    return first + second


def send_kernel(spectrum, out):
    for c in range(2):
        a = spectrum[c, 0].reshape(32, 8, 128)
        b = spectrum[c, 1].reshape(32, 8, 128)
        low = lax.broadcasted_iota(jnp.int32, a.shape, 1) < 4
        out[:, 0, c] = jnp.where(low, a, pltpu.roll(b, 4, 1))
        out[:, 1, c] = jnp.where(low, pltpu.roll(a, 4, 1), b)


def update_kernel(arrived, spectrum, out):
    for c in range(2):
        a = arrived[:, 0, c]
        b = arrived[:, 1, c]
        low = lax.broadcasted_iota(jnp.int32, a.shape, 1) < 4
        first = jnp.where(low, a, pltpu.roll(b, 4, 1)).reshape(256, 128)
        second = jnp.where(low, pltpu.roll(a, 4, 1), b).reshape(256, 128)
        out[c, 0] = spectrum[c, 0] + step_size * first
        out[c, 1] = spectrum[c, 1] + step_size * second


def pack_kernel(measured, weights, out):
    for k in range(3):
        pieces = []
        for q in range(4):
            for f0 in range(2):
                rows = pl.ds(q * 64, 64)
                pieces.append(measured[k, f0, rows, :] if k < 2 else weights[rows, :])
        for d, piece in enumerate(swap_groups(pieces, 16)):
            out[d, k * 64 : (k + 1) * 64, :] = piece


def unpack_kernel(arrived, out):
    for k in range(2):
        pieces = [arrived[d, k * 64 : (k + 1) * 64, :] for d in range(8)]
        for g, piece in enumerate(swap_groups(pieces, 16)):
            out[k, g % 2, pl.ds(g // 2 * 64, 64), :] = piece


def pair_kernel(arrived, turn, twist, table_high, table_low, out):
    low = lax.broadcasted_iota(jnp.int32, (8, 128), 0) < 4
    for y in range(4):
        points = []
        for z in range(16):
            wr, wi = turn[0, z, y], turn[1, z, y]
            pr = pi = None
            for layer in range(7, -1, -1):
                re, im = arrived[z, layer // 2, 0], arrived[z, layer // 2, 1]
                if layer % 2:
                    re = jnp.where(low, pltpu.roll(re, 4, 0), re)
                    im = jnp.where(low, pltpu.roll(im, 4, 0), im)
                else:
                    re = jnp.where(low, re, pltpu.roll(re, 4, 0))
                    im = jnp.where(low, im, pltpu.roll(im, 4, 0))
                if pr is not None:
                    re, im = re + (pr * wr + pi * wi), im + (pi * wr - pr * wi)
                pr, pi = re, im
            points.append((pr * wr + pi * wi, pi * wr - pr * wi))
        points = sixteen(points, 1)
        res, ims = [], []
        for r0, (re, im) in enumerate(points):
            tr, ti = twist[0, r0], twist[1, r0]
            res.append(re * tr - im * ti)
            ims.append(re * ti + im * tr)
        both = jnp.concatenate([jnp.concatenate(res, 0), jnp.concatenate(ims, 0)], 1)
        high, rest = split(both)
        stacked = jnp.concatenate([high, rest], 0)
        first = lax.dot_general(table_high[...], stacked, nt_form, preferred_element_type=f32)
        second = lax.dot_general(table_low[...], high, nt_form, preferred_element_type=f32)
        done = first[:, :128] + first[:, 128:] + second
        for c in range(2):
            out[pl.ds(y * 2 + c, 128, stride=8), :] = done[c * 128 : (c + 1) * 128]


def gradient_kernel(arrived, turn, twist, table_high, table_low, out, points):
    for y in range(4):
        re = arrived[pl.ds(y * 2, 128, stride=8), :]
        im = arrived[pl.ds(y * 2 + 1, 128, stride=8), :]
        both = jnp.concatenate([re.T, im.T], 1)
        high, rest = split(both)
        first = dot(jnp.concatenate([high, rest], 0), table_high[...])
        done = first[:128] + first[128:] + dot(high, table_low[...])
        values = []
        for r0 in range(16):
            re = done[r0 * 8 : (r0 + 1) * 8, :128]
            im = done[r0 * 8 : (r0 + 1) * 8, 128:]
            tr, ti = twist[0, r0], twist[1, r0]
            values.append((re * tr + im * ti, im * tr - re * ti))
        for z, (re, im) in enumerate(sixteen(values, -1)):
            points[y, z, 0] = re
            points[y, z, 1] = im
    low = lax.broadcasted_iota(jnp.int32, (8, 128), 0) < 4
    for z in range(16):
        sums = [None] * 8
        for y in range(4):
            wr, wi = turn[0, z, y], turn[1, z, y]
            re, im = points[y, z, 0], points[y, z, 1]
            for layer in range(8):
                re, im = re * wr - im * wi, im * wr + re * wi
                if sums[layer] is None:
                    sums[layer] = (re, im)
                else:
                    sums[layer] = (sums[layer][0] + re, sums[layer][1] + im)
        for y in range(4):
            for c in range(2):
                a, b = sums[2 * y][c], sums[2 * y + 1][c]
                x = jnp.where(low, a, pltpu.roll(b, 4, 0))
                w = jnp.where(low, pltpu.roll(a, 4, 0), b)
                out[z, y, c] = x + w


def middle_kernel(
    arrived,
    echoes,
    twist,
    mix,
    mix_back,
    long_high,
    long_low,
    back_high,
    back_low,
    out,
    resid,
):
    high, rest = split(arrived[...])
    first = dot(long_high[...], jnp.concatenate([high, rest], 1))
    done = first[:, :128] + first[:, 128:] + dot(long_low[...], high)
    re, im = done[:512], done[512:]
    tr, ti = twist[0], twist[1]
    both = jnp.concatenate([re * tr - im * ti, re * ti + im * tr], 1)
    high, rest = split(both)
    field = dot(high, mix[...]) + dot(rest, mix[...])
    parts = []
    for k in range(3):
        rows = []
        for odd in range(2):
            pieces = [echoes[2 * t1 + odd, k * 64 : (k + 1) * 64, :] for t1 in range(4)]
            rows += swap_groups(pieces, 32)
        parts.append(jnp.concatenate(rows, 0))
    left = []
    for k in range(2):
        value = parts[2] * (parts[k] - field[:, k * 128 : (k + 1) * 128])
        left.append(value)
        for odd in range(2):
            pieces = [value[odd * 256 + q * 64 : odd * 256 + (q + 1) * 64] for q in range(4)]
            for t1, piece in enumerate(swap_groups(pieces, 32)):
                resid[2 * t1 + odd, k * 64 : (k + 1) * 64, :] = piece
    high, rest = split(jnp.concatenate(left, 1))
    mixed = dot(high, mix_back[...]) + dot(rest, mix_back[...])
    re, im = mixed[:, :128], mixed[:, 128:]
    both = jnp.concatenate([re * tr + im * ti, im * tr - re * ti], 0)
    high, rest = split(both)
    first = dot(back_high[...], jnp.concatenate([high, rest], 1))
    out[...] = first[:, :128] + first[:, 128:] + dot(back_low[...], high)


def call(kernel, shapes, *operands, scratch=(), flops=0):
    single = not isinstance(shapes, list)
    shapes = [shapes] if single else shapes
    spec = pl.BlockSpec(memory_space=pltpu.VMEM)
    bytes_moved = sum(math.prod(s) * 4 for s in shapes) + sum(
        o.size * o.dtype.itemsize for o in operands
    )
    out = pl.pallas_call(
        kernel,
        out_shape=[jax.ShapeDtypeStruct(s, f32) for s in shapes],
        in_specs=[spec] * len(operands),
        out_specs=[spec] * len(shapes),
        scratch_shapes=list(scratch),
        compiler_params=params,
        cost_estimate=pl.CostEstimate(
            flops=flops, bytes_accessed=bytes_moved, transcendentals=0
        ),
    )(*operands)
    return out[0] if single else out


def exchange(value, axes):
    return lax.all_to_all(value, axes, split_axis=0, concat_axis=0, tiled=True)


def wave_numbers(indices, total):
    signed = jnp.where(indices < total // 2, indices, indices - total)
    return 2.0 * jnp.pi / total * signed.astype(f32)


def turns(wavenumber, tx, z, y):
    low = jnp.arange(8, dtype=jnp.int32) % 4
    sent = wave_numbers(tx * 256 + z * 16 + y * 4 + low, 2048)
    heard = wave_numbers(jnp.arange(2048, dtype=jnp.int32).reshape(16, 1, 1, 128), 2048)
    waves = jnp.repeat(wavenumber.reshape(4, 2), 4, axis=1)
    squared = waves * waves
    first = jnp.sqrt(jnp.maximum(squared - (sent * sent)[None, :], 0.0) + root_floor)
    second = jnp.sqrt(
        jnp.maximum(squared[None, :, :, None] - heard * heard, 0.0) + root_floor
    )
    phase = depth_step * (first[None, :, :, None] + second)
    return jnp.stack([jnp.cos(phase), jnp.sin(phase)])


def per_device(spectrum, measured, wavenumber, send_weight, hear_weight, aperture):
    table = tables()
    tx, z, y = lax.axis_index("tx"), lax.axis_index("rx"), lax.axis_index("freq")

    sent = call(send_kernel, (32, 2, 2, 8, 128), spectrum)
    arrived = exchange(sent.reshape(64, 16, 128), ("rx", "freq"))

    turn = turns(wavenumber, tx, z, y)
    gate = aperture.astype(f32)
    weights = (
        send_weight.reshape(16, 16, 1, 1)
        * gate.reshape(16, 1, 8, 1)
        * hear_weight.reshape(1, 1, 8, 16)
    ).reshape(256, 128)
    echoes = exchange(call(pack_kernel, (8, 192, 128), measured, weights), "tx")

    pairs = call(
        pair_kernel,
        (1024, 128),
        arrived.reshape(16, 4, 2, 8, 128),
        turn,
        table["twist_heard"],
        *table["lanes"],
        flops=10**9,
    )
    columns = exchange(pairs.reshape(512, 2, 128), ("rx", "tx", "freq")).reshape(1024, 128)
    back, resid = call(
        middle_kernel,
        [(1024, 128), (8, 128, 128)],
        columns,
        echoes,
        table["twist_sent"],
        table["mix"],
        table["mix_back"],
        *table["long"],
        *table["long_back"],
        flops=3 * 10**9,
    )
    rows = exchange(back.reshape(512, 2, 128), ("rx", "tx", "freq")).reshape(1024, 128)
    residual = call(unpack_kernel, (2, 2, 256, 128), exchange(resid, "tx"))
    gradient = call(
        gradient_kernel,
        (16, 4, 2, 8, 128),
        rows,
        turn,
        table["twist_heard"],
        *table["lanes"],
        scratch=[pltpu.VMEM((4, 16, 2, 8, 128), f32)],
        flops=10**9,
    )
    gathered = exchange(gradient.reshape(64, 16, 128), ("rx", "freq"))
    updated = call(
        update_kernel, (2, 2, 256, 128), gathered.reshape(32, 2, 2, 8, 128), spectrum
    )
    return updated, residual


def solution(mesh):
    placed = (
        P(None, "freq", "tx", "rx"),
        P(None, "freq", "tx", "rx"),
        P(),
        P("tx"),
        P("rx"),
        P("tx", "rx"),
    )
    return jax.shard_map(
        per_device,
        mesh=mesh,
        in_specs=placed,
        out_specs=(P(None, "freq", "tx", "rx"), P(None, "freq", "tx", "rx")),
        check_vma=False,
    )
```

```python
import functools
import math

import jax
import jax.numpy as jnp
import ml_dtypes
import numpy as np
from jax import lax
from jax.experimental import pallas as pl
from jax.experimental.pallas import tpu as pltpu
from jax.sharding import PartitionSpec as P

depth_step = 2.0
step_size = 0.125
root_floor = 0.25
bf16 = jnp.bfloat16
f32 = jnp.float32
nt_form = (((1,), (1,)), ((), ()))
params = pltpu.CompilerParams(vmem_limit_bytes=56 * 1024 * 1024)


def halves(table):
    high = table.astype(np.float32).astype(ml_dtypes.bfloat16)
    low = (table - high.astype(np.float64)).astype(np.float32).astype(ml_dtypes.bfloat16)
    return high, low


def angles(left, right, total):
    return 2.0 * np.pi / total * ((left[:, None] * right[None, :]) % total)


@functools.cache
def tables():
    index = np.arange(128)
    order = index.reshape(16, 8).T.reshape(-1)
    theta = angles(order, index, 128)
    scale = 1.0 / math.sqrt(2048.0)
    cosine, sine = np.cos(theta) * scale, np.sin(theta) * scale
    lanes = np.block([[cosine, -sine], [sine, cosine]])
    theta = angles(np.arange(16), index, 2048)
    twist_heard = np.stack([np.cos(theta), np.sin(theta)])
    twist_heard = np.broadcast_to(twist_heard[:, :, None, :], (2, 16, 8, 128)).astype(np.float32)
    index = np.arange(512)
    theta = angles(index, index, 512)
    long = halves(np.cos(theta) * scale) + halves(np.sin(theta) * scale)
    low_of_lane = np.arange(128) % 4
    theta = angles(np.arange(512), low_of_lane, 2048)
    twist_sent = np.stack([np.cos(theta), np.sin(theta)]).astype(np.float32)
    mix = np.zeros((2, 16, 2, 4, 2, 4, 2, 16))
    quarter = ((1, 0), (0, 1), (-1, 0), (0, -1))
    for r0 in range(16):
        for f0 in range(2):
            for mi in range(4):
                for t1 in range(4):
                    c, s = quarter[mi * t1 % 4]
                    mix[0, r0, f0, mi, 0, t1, f0, r0] = c
                    mix[1, r0, f0, mi, 0, t1, f0, r0] = -s
                    mix[0, r0, f0, mi, 1, t1, f0, r0] = s
                    mix[1, r0, f0, mi, 1, t1, f0, r0] = c
    mix = mix.reshape(256, 256).astype(ml_dtypes.bfloat16)
    return dict(
        lanes=halves(lanes),
        twist_heard=twist_heard,
        long=long,
        twist_sent=twist_sent,
        mix=mix,
        mix_back=mix.T.copy(),
    )


def split(value):
    high = value.astype(bf16)
    return high, (value - high.astype(f32)).astype(bf16)


def dot(left, right):
    return jnp.dot(left, right, preferred_element_type=f32)


def swap_groups(arrays, width):
    arrays = list(arrays)
    group = lax.broadcasted_iota(jnp.int32, arrays[0].shape, 1) // width
    bit = 1
    while bit < len(arrays):
        high = (group & bit) != 0
        for i in range(len(arrays)):
            if i & bit:
                continue
            a, b = arrays[i], arrays[i | bit]
            arrays[i] = jnp.where(high, pltpu.roll(b, bit * width, 1), a)
            arrays[i | bit] = jnp.where(high, b, pltpu.roll(a, 128 - bit * width, 1))
        bit *= 2
    return arrays


def times(value, c, s):
    re, im = value
    if (c, s) == (1, 0):
        return value
    if (c, s) == (0, 1):
        return -im, re
    if (c, s) == (0, -1):
        return im, -re
    if (c, s) == (-1, 0):
        return -re, -im
    return re * c - im * s, re * s + im * c


def sixteen(values, sign):
    count = len(values)
    if count == 1:
        return values
    even = sixteen(values[0::2], sign)
    odd = sixteen(values[1::2], sign)
    first, second = [], []
    for k in range(count // 2):
        if 4 * k == 0:
            turn = (1, 0)
        elif 4 * k == count:
            turn = (0, sign)
        else:
            angle = 2.0 * math.pi * k / count
            turn = (math.cos(angle), sign * math.sin(angle))
        a, b = even[k], times(odd[k], *turn)
        first.append((a[0] + b[0], a[1] + b[1]))
        second.append((a[0] - b[0], a[1] - b[1]))
    return first + second


def send_kernel(spectrum, out):
    for c in range(2):
        a = spectrum[c, 0].reshape(32, 8, 128)
        b = spectrum[c, 1].reshape(32, 8, 128)
        low = lax.broadcasted_iota(jnp.int32, a.shape, 1) < 4
        out[:, 0, c] = jnp.where(low, a, pltpu.roll(b, 4, 1))
        out[:, 1, c] = jnp.where(low, pltpu.roll(a, 4, 1), b)


def update_kernel(arrived, spectrum, out):
    for c in range(2):
        a = arrived[:, 0, c]
        b = arrived[:, 1, c]
        low = lax.broadcasted_iota(jnp.int32, a.shape, 1) < 4
        first = jnp.where(low, a, pltpu.roll(b, 4, 1)).reshape(256, 128)
        second = jnp.where(low, pltpu.roll(a, 4, 1), b).reshape(256, 128)
        out[c, 0] = spectrum[c, 0] + step_size * first
        out[c, 1] = spectrum[c, 1] + step_size * second


def pack_kernel(place, measured, weights, *refs):
    *outs, held = refs
    for k in range(3):
        pieces = []
        for q in range(4):
            for f0 in range(2):
                rows = pl.ds(q * 64, 64)
                pieces.append(measured[k, f0, rows, :] if k < 2 else weights[rows, :])
        for d, piece in enumerate(swap_groups(pieces, 16)):
            held[d, k * 64 : (k + 1) * 64, :] = piece
    for step in range(8):
        outs[step][...] = held[(place[0] + step) & 7]


def unpack_kernel(place, *refs):
    *arrived, out, held = refs
    for step in range(8):
        held[(place[0] + 8 - step) & 7] = arrived[step][...]
    for k in range(2):
        pieces = [held[d, k * 64 : (k + 1) * 64, :] for d in range(8)]
        for g, piece in enumerate(swap_groups(pieces, 16)):
            out[k, g % 2, pl.ds(g // 2 * 64, 64), :] = piece


def pair_kernel(arrived, turn, twist, table_high, table_low, out):
    low = lax.broadcasted_iota(jnp.int32, (8, 128), 0) < 4
    for y in range(4):
        points = []
        for z in range(16):
            wr, wi = turn[0, z, y], turn[1, z, y]
            pr = pi = None
            for layer in range(7, -1, -1):
                re, im = arrived[z, layer // 2, 0], arrived[z, layer // 2, 1]
                if layer % 2:
                    re = jnp.where(low, pltpu.roll(re, 4, 0), re)
                    im = jnp.where(low, pltpu.roll(im, 4, 0), im)
                else:
                    re = jnp.where(low, re, pltpu.roll(re, 4, 0))
                    im = jnp.where(low, im, pltpu.roll(im, 4, 0))
                if pr is not None:
                    re, im = re + (pr * wr + pi * wi), im + (pi * wr - pr * wi)
                pr, pi = re, im
            points.append((pr * wr + pi * wi, pi * wr - pr * wi))
        points = sixteen(points, 1)
        res, ims = [], []
        for r0, (re, im) in enumerate(points):
            tr, ti = twist[0, r0], twist[1, r0]
            res.append(re * tr - im * ti)
            ims.append(re * ti + im * tr)
        both = jnp.concatenate([jnp.concatenate(res, 0), jnp.concatenate(ims, 0)], 1)
        high, rest = split(both)
        stacked = jnp.concatenate([high, rest], 0)
        first = lax.dot_general(table_high[...], stacked, nt_form, preferred_element_type=f32)
        second = lax.dot_general(table_low[...], high, nt_form, preferred_element_type=f32)
        done = first[:, :128] + first[:, 128:] + second
        for c in range(2):
            out[pl.ds(y * 2 + c, 128, stride=8), :] = done[c * 128 : (c + 1) * 128]


def gradient_kernel(arrived, turn, twist, table_high, table_low, out, points):
    for y in range(4):
        re = arrived[pl.ds(y * 2, 128, stride=8), :]
        im = arrived[pl.ds(y * 2 + 1, 128, stride=8), :]
        both = jnp.concatenate([re.T, im.T], 1)
        high, rest = split(both)
        first = dot(jnp.concatenate([high, rest], 0), table_high[...])
        done = first[:128] + first[128:] + dot(high, table_low[...])
        values = []
        for r0 in range(16):
            re = done[r0 * 8 : (r0 + 1) * 8, :128]
            im = done[r0 * 8 : (r0 + 1) * 8, 128:]
            tr, ti = twist[0, r0], twist[1, r0]
            values.append((re * tr + im * ti, im * tr - re * ti))
        for z, (re, im) in enumerate(sixteen(values, -1)):
            points[y, z, 0] = re
            points[y, z, 1] = im
    low = lax.broadcasted_iota(jnp.int32, (8, 128), 0) < 4
    for z in range(16):
        sums = [None] * 8
        for y in range(4):
            wr, wi = turn[0, z, y], turn[1, z, y]
            re, im = points[y, z, 0], points[y, z, 1]
            for layer in range(8):
                re, im = re * wr - im * wi, im * wr + re * wi
                if sums[layer] is None:
                    sums[layer] = (re, im)
                else:
                    sums[layer] = (sums[layer][0] + re, sums[layer][1] + im)
        for y in range(4):
            for c in range(2):
                a, b = sums[2 * y][c], sums[2 * y + 1][c]
                x = jnp.where(low, a, pltpu.roll(b, 4, 0))
                w = jnp.where(low, pltpu.roll(a, 4, 0), b)
                out[z, y, c] = x + w


def long_sums(re, im, tables_of):
    re_high, re_low = split(re)
    im_high, im_low = split(im)
    whole = jnp.concatenate([re_high, re_low, im_high, im_low], 1)
    high = jnp.concatenate([re_high, im_high], 1)
    sums = []
    for k in range(2):
        first = dot(tables_of[2 * k][...], whole)
        second = dot(tables_of[2 * k + 1][...], high)
        sums.append(first[:, :128] + first[:, 128:256] + second[:, :128])
        sums.append(first[:, 256:384] + first[:, 384:] + second[:, 128:])
    return sums


def middle_kernel(place, arrived, twist, mix, mix_back, *refs):
    long, echoes, out, sent = refs[:4], refs[4:12], refs[12], refs[13:21]
    held, resid = refs[21:]
    for step in range(8):
        held[(place[0] + 8 - step) & 7] = echoes[step][...]
    cos_re, cos_im, sin_re, sin_im = long_sums(
        arrived[pl.ds(0, 512, stride=2), :], arrived[pl.ds(1, 512, stride=2), :], long
    )
    re, im = cos_re - sin_im, sin_re + cos_im
    tr, ti = twist[0], twist[1]
    both = jnp.concatenate([re * tr - im * ti, re * ti + im * tr], 1)
    high, rest = split(both)
    field = dot(high, mix[...]) + dot(rest, mix[...])
    parts = []
    for k in range(3):
        rows = []
        for odd in range(2):
            pieces = [held[2 * t1 + odd, k * 64 : (k + 1) * 64, :] for t1 in range(4)]
            rows += swap_groups(pieces, 32)
        parts.append(jnp.concatenate(rows, 0))
    left = []
    for k in range(2):
        value = parts[2] * (parts[k] - field[:, k * 128 : (k + 1) * 128])
        left.append(value)
        for odd in range(2):
            pieces = [value[odd * 256 + q * 64 : odd * 256 + (q + 1) * 64] for q in range(4)]
            for t1, piece in enumerate(swap_groups(pieces, 32)):
                resid[2 * t1 + odd, k * 64 : (k + 1) * 64, :] = piece
    for step in range(8):
        sent[step][...] = resid[(place[0] + step) & 7]
    high, rest = split(jnp.concatenate(left, 1))
    mixed = dot(high, mix_back[...]) + dot(rest, mix_back[...])
    re, im = mixed[:, :128], mixed[:, 128:]
    cos_re, cos_im, sin_re, sin_im = long_sums(re * tr + im * ti, im * tr - re * ti, long)
    out[pl.ds(0, 512, stride=2), :] = cos_re + sin_im
    out[pl.ds(1, 512, stride=2), :] = cos_im - sin_re


def call(kernel, shapes, *operands, scratch=(), place=None, flops=0):
    single = not isinstance(shapes, list)
    shapes = [shapes] if single else shapes
    spec = pl.BlockSpec(memory_space=pltpu.VMEM)
    in_specs = [spec] * len(operands)
    bytes_moved = sum(math.prod(s) * 4 for s in shapes) + sum(
        o.size * o.dtype.itemsize for o in operands
    )
    if place is not None:
        operands = (place, *operands)
        in_specs = [pl.BlockSpec(memory_space=pltpu.SMEM), *in_specs]
    out = pl.pallas_call(
        kernel,
        out_shape=[jax.ShapeDtypeStruct(s, f32) for s in shapes],
        in_specs=in_specs,
        out_specs=[spec] * len(shapes),
        scratch_shapes=[pltpu.VMEM(s, f32) for s in scratch],
        compiler_params=params,
        cost_estimate=pl.CostEstimate(
            flops=flops, bytes_accessed=bytes_moved, transcendentals=0
        ),
    )(*operands)
    return out[0] if single else out


def exchange(value, axes):
    return lax.all_to_all(value, axes, split_axis=0, concat_axis=0, tiled=True)


def along_tx(pieces):
    moved = [pieces[0]]
    for step in range(1, 8):
        moved.append(lax.ppermute(pieces[step], "tx", [(i, (i + step) % 8) for i in range(8)]))
    return moved


def wave_numbers(indices, total):
    signed = jnp.where(indices < total // 2, indices, indices - total)
    return 2.0 * jnp.pi / total * signed.astype(f32)


def turns(wavenumber, tx, z, y):
    low = jnp.arange(8, dtype=jnp.int32) % 4
    sent = wave_numbers(tx * 256 + z * 16 + y * 4 + low, 2048)
    heard = wave_numbers(jnp.arange(2048, dtype=jnp.int32).reshape(16, 1, 1, 128), 2048)
    waves = jnp.repeat(wavenumber.reshape(4, 2), 4, axis=1)
    squared = waves * waves
    first = jnp.sqrt(jnp.maximum(squared - (sent * sent)[None, :], 0.0) + root_floor)
    second = jnp.sqrt(
        jnp.maximum(squared[None, :, :, None] - heard * heard, 0.0) + root_floor
    )
    phase = depth_step * (first[None, :, :, None] + second)
    return jnp.stack([jnp.cos(phase), jnp.sin(phase)])


def per_device(spectrum, measured, wavenumber, send_weight, hear_weight, aperture):
    table = tables()
    tx, z, y = lax.axis_index("tx"), lax.axis_index("rx"), lax.axis_index("freq")

    sent = call(send_kernel, (32, 2, 2, 8, 128), spectrum)
    arrived = exchange(sent.reshape(64, 16, 128), ("rx", "freq"))

    turn = turns(wavenumber, tx, z, y)
    gate = aperture.astype(f32)
    weights = (
        send_weight.reshape(16, 16, 1, 1)
        * gate.reshape(16, 1, 8, 1)
        * hear_weight.reshape(1, 1, 8, 16)
    ).reshape(256, 128)
    place = tx.astype(jnp.int32).reshape(1)
    echoes = along_tx(
        call(
            pack_kernel,
            [(192, 128)] * 8,
            measured,
            weights,
            scratch=[(8, 192, 128)],
            place=place,
        )
    )

    pairs = call(
        pair_kernel,
        (1024, 128),
        arrived.reshape(16, 4, 2, 8, 128),
        turn,
        table["twist_heard"],
        *table["lanes"],
        flops=10**9,
    )
    columns = exchange(pairs.reshape(512, 2, 128), ("tx", "rx", "freq")).reshape(1024, 128)
    back, *resid = call(
        middle_kernel,
        [(1024, 128)] + [(128, 128)] * 8,
        columns,
        table["twist_sent"],
        table["mix"],
        table["mix_back"],
        *table["long"],
        *echoes,
        scratch=[(8, 192, 128), (8, 128, 128)],
        place=place,
        flops=3 * 10**9,
    )
    rows = exchange(back.reshape(512, 2, 128), ("tx", "rx", "freq")).reshape(1024, 128)
    residual = call(
        unpack_kernel,
        (2, 2, 256, 128),
        *along_tx(resid),
        scratch=[(8, 128, 128)],
        place=place,
    )
    gradient = call(
        gradient_kernel,
        (16, 4, 2, 8, 128),
        rows,
        turn,
        table["twist_heard"],
        *table["lanes"],
        scratch=[(4, 16, 2, 8, 128)],
        flops=10**9,
    )
    gathered = exchange(gradient.reshape(64, 16, 128), ("rx", "freq"))
    updated = call(
        update_kernel, (2, 2, 256, 128), gathered.reshape(32, 2, 2, 8, 128), spectrum
    )
    return updated, residual


def solution(mesh):
    placed = (
        P(None, "freq", "tx", "rx"),
        P(None, "freq", "tx", "rx"),
        P(),
        P("tx"),
        P("rx"),
        P("tx", "rx"),
    )
    return jax.shard_map(
        per_device,
        mesh=mesh,
        in_specs=placed,
        out_specs=(P(None, "freq", "tx", "rx"), P(None, "freq", "tx", "rx")),
        check_vma=False,
    )
```

```python
import functools
import math

import jax
import jax.numpy as jnp
import ml_dtypes
import numpy as np
from jax import lax
from jax.experimental import pallas as pl
from jax.experimental.pallas import tpu as pltpu
from jax.sharding import PartitionSpec as P

depth_step = 2.0
step_size = 0.125
root_floor = 0.25
early_echoes = 3
early_pieces = 5
bf16 = jnp.bfloat16
f32 = jnp.float32
nt_form = (((1,), (1,)), ((), ()))
params = pltpu.CompilerParams(vmem_limit_bytes=24 * 1024 * 1024)


def halves(table):
    high = table.astype(np.float32).astype(ml_dtypes.bfloat16)
    low = (table - high.astype(np.float64)).astype(np.float32).astype(ml_dtypes.bfloat16)
    return high, low


def angles(left, right, total):
    return 2.0 * np.pi / total * ((left[:, None] * right[None, :]) % total)


@functools.cache
def tables():
    index = np.arange(128)
    order = index.reshape(16, 8).T.reshape(-1)
    theta = angles(order, index, 128)
    scale = 1.0 / math.sqrt(2048.0)
    cosine, sine = np.cos(theta) * scale, np.sin(theta) * scale
    lanes = np.block([[cosine, -sine], [sine, cosine]])
    theta = angles(np.arange(16), index, 2048)
    twist_heard = np.stack([np.cos(theta), np.sin(theta)])
    twist_heard = np.broadcast_to(twist_heard[:, :, None, :], (2, 16, 8, 128)).astype(np.float32)
    index = np.arange(512)
    theta = angles(index, index, 512)
    long = halves(np.cos(theta) * scale) + halves(np.sin(theta) * scale)
    low_of_lane = np.arange(128) % 4
    theta = angles(np.arange(512), low_of_lane, 2048)
    twist_sent = np.stack([np.cos(theta), np.sin(theta)]).astype(np.float32)
    mix = np.zeros((2, 16, 2, 4, 2, 4, 2, 16))
    quarter = ((1, 0), (0, 1), (-1, 0), (0, -1))
    for r0 in range(16):
        for f0 in range(2):
            for mi in range(4):
                for t1 in range(4):
                    c, s = quarter[mi * t1 % 4]
                    mix[0, r0, f0, mi, 0, t1, f0, r0] = c
                    mix[1, r0, f0, mi, 0, t1, f0, r0] = -s
                    mix[0, r0, f0, mi, 1, t1, f0, r0] = s
                    mix[1, r0, f0, mi, 1, t1, f0, r0] = c
    mix = mix.reshape(256, 256).astype(ml_dtypes.bfloat16)
    return dict(
        lanes=halves(lanes),
        twist_heard=twist_heard,
        long=long,
        twist_sent=twist_sent,
        mix=mix,
        mix_back=mix.T.copy(),
    )


def split(value):
    high = value.astype(bf16)
    return high, (value - high.astype(f32)).astype(bf16)


def dot(left, right):
    return jnp.dot(left, right, preferred_element_type=f32)


def swap_groups(arrays, width):
    arrays = list(arrays)
    group = lax.broadcasted_iota(jnp.int32, arrays[0].shape, 1) // width
    bit = 1
    while bit < len(arrays):
        high = (group & bit) != 0
        for i in range(len(arrays)):
            if i & bit:
                continue
            a, b = arrays[i], arrays[i | bit]
            arrays[i] = jnp.where(high, pltpu.roll(b, bit * width, 1), a)
            arrays[i | bit] = jnp.where(high, b, pltpu.roll(a, 128 - bit * width, 1))
        bit *= 2
    return arrays


def times(value, c, s):
    re, im = value
    if (c, s) == (1, 0):
        return value
    if (c, s) == (0, 1):
        return -im, re
    if (c, s) == (0, -1):
        return im, -re
    if (c, s) == (-1, 0):
        return -re, -im
    return re * c - im * s, re * s + im * c


def sixteen(values, sign):
    count = len(values)
    if count == 1:
        return values
    even = sixteen(values[0::2], sign)
    odd = sixteen(values[1::2], sign)
    first, second = [], []
    for k in range(count // 2):
        if 4 * k == 0:
            turn = (1, 0)
        elif 4 * k == count:
            turn = (0, sign)
        else:
            angle = 2.0 * math.pi * k / count
            turn = (math.cos(angle), sign * math.sin(angle))
        a, b = even[k], times(odd[k], *turn)
        first.append((a[0] + b[0], a[1] + b[1]))
        second.append((a[0] - b[0], a[1] - b[1]))
    return first + second


def send_kernel(spectrum, out):
    for c in range(2):
        a = spectrum[c, 0].reshape(32, 8, 128)
        b = spectrum[c, 1].reshape(32, 8, 128)
        low = lax.broadcasted_iota(jnp.int32, a.shape, 1) < 4
        out[:, 0, c] = jnp.where(low, a, pltpu.roll(b, 4, 1))
        out[:, 1, c] = jnp.where(low, pltpu.roll(a, 4, 1), b)


def update_kernel(arrived, spectrum, out):
    for c in range(2):
        a = arrived[:, 0, c]
        b = arrived[:, 1, c]
        low = lax.broadcasted_iota(jnp.int32, a.shape, 1) < 4
        first = jnp.where(low, a, pltpu.roll(b, 4, 1)).reshape(256, 128)
        second = jnp.where(low, pltpu.roll(a, 4, 1), b).reshape(256, 128)
        out[c, 0] = spectrum[c, 0] + step_size * first
        out[c, 1] = spectrum[c, 1] + step_size * second


def pack_kernel(place, measured, send, hear, gate, *refs):
    *outs, held = refs
    tile = lax.broadcasted_iota(jnp.int32, (256, 16), 0) // 16
    down = (tile == lax.broadcasted_iota(jnp.int32, (256, 16), 1)).astype(bf16)
    tile = lax.broadcasted_iota(jnp.int32, (8, 128), 1) // 16
    along = (tile == lax.broadcasted_iota(jnp.int32, (8, 128), 0)).astype(bf16)
    live = dot(dot(down, gate[...].astype(f32).astype(bf16)).astype(bf16), along)
    columns = [jnp.broadcast_to(send[k : k + 1, :], (128, 128)).T for k in range(2)]
    weights = jnp.concatenate(columns, 0) * hear[...] * live
    for k in range(3):
        pieces = []
        for q in range(4):
            for f0 in range(2):
                rows = slice(q * 64, (q + 1) * 64)
                pieces.append(measured[k, f0, rows, :] if k < 2 else weights[rows])
        for d, piece in enumerate(swap_groups(pieces, 16)):
            held[d, k * 64 : (k + 1) * 64, :] = piece
    for step in range(8):
        outs[step][...] = held[(place[0] + step) & 7]


def unpack_kernel(place, *refs):
    *arrived, out, held = refs
    for step in range(8):
        held[(place[0] + 8 - step) & 7] = arrived[step][...]
    for k in range(2):
        pieces = [held[d, k * 64 : (k + 1) * 64, :] for d in range(8)]
        for g, piece in enumerate(swap_groups(pieces, 16)):
            out[k, g % 2, pl.ds(g // 2 * 64, 64), :] = piece


def pair_kernel(arrived, turn, twist, table_high, table_low, *refs):
    out = refs[-1]
    low = lax.broadcasted_iota(jnp.int32, (8, 128), 0) < 4
    for y in range(4):
        points = []
        for z in range(16):
            wr, wi = turn[0, z, y], turn[1, z, y]
            pr = pi = None
            for layer in range(7, -1, -1):
                re, im = arrived[z, layer // 2, 0], arrived[z, layer // 2, 1]
                if layer % 2:
                    re = jnp.where(low, pltpu.roll(re, 4, 0), re)
                    im = jnp.where(low, pltpu.roll(im, 4, 0), im)
                else:
                    re = jnp.where(low, re, pltpu.roll(re, 4, 0))
                    im = jnp.where(low, im, pltpu.roll(im, 4, 0))
                if pr is not None:
                    re, im = re + (pr * wr + pi * wi), im + (pi * wr - pr * wi)
                pr, pi = re, im
            points.append((pr * wr + pi * wi, pi * wr - pr * wi))
        points = sixteen(points, 1)
        res, ims = [], []
        for r0, (re, im) in enumerate(points):
            tr, ti = twist[0, r0], twist[1, r0]
            res.append(re * tr - im * ti)
            ims.append(re * ti + im * tr)
        both = jnp.concatenate([jnp.concatenate(res, 0), jnp.concatenate(ims, 0)], 1)
        high, rest = split(both)
        stacked = jnp.concatenate([high, rest], 0)
        first = lax.dot_general(table_high[...], stacked, nt_form, preferred_element_type=f32)
        second = lax.dot_general(table_low[...], high, nt_form, preferred_element_type=f32)
        done = first[:, :128] + first[:, 128:] + second
        for c in range(2):
            out[pl.ds(y * 2 + c, 128, stride=8), :] = done[c * 128 : (c + 1) * 128]


def gradient_kernel(arrived, turn, twist, table_high, table_low, *refs):
    out, points = refs[-2:]
    for y in range(4):
        re = arrived[pl.ds(y * 2, 128, stride=8), :]
        im = arrived[pl.ds(y * 2 + 1, 128, stride=8), :]
        both = jnp.concatenate([re.T, im.T], 1)
        high, rest = split(both)
        first = dot(jnp.concatenate([high, rest], 0), table_high[...])
        done = first[:128] + first[128:] + dot(high, table_low[...])
        values = []
        for r0 in range(16):
            re = done[r0 * 8 : (r0 + 1) * 8, :128]
            im = done[r0 * 8 : (r0 + 1) * 8, 128:]
            tr, ti = twist[0, r0], twist[1, r0]
            values.append((re * tr + im * ti, im * tr - re * ti))
        for z, (re, im) in enumerate(sixteen(values, -1)):
            points[y, z, 0] = re
            points[y, z, 1] = im
    low = lax.broadcasted_iota(jnp.int32, (8, 128), 0) < 4
    for z in range(16):
        sums = [None] * 8
        for y in range(4):
            wr, wi = turn[0, z, y], turn[1, z, y]
            re, im = points[y, z, 0], points[y, z, 1]
            for layer in range(8):
                re, im = re * wr - im * wi, im * wr + re * wi
                if sums[layer] is None:
                    sums[layer] = (re, im)
                else:
                    sums[layer] = (sums[layer][0] + re, sums[layer][1] + im)
        for y in range(4):
            for c in range(2):
                a, b = sums[2 * y][c], sums[2 * y + 1][c]
                x = jnp.where(low, a, pltpu.roll(b, 4, 0))
                w = jnp.where(low, pltpu.roll(a, 4, 0), b)
                out[z, y, c] = x + w


def long_sums(re, im, tables_of):
    re_high, re_low = split(re)
    im_high, im_low = split(im)
    whole = jnp.concatenate([re_high, re_low, im_high, im_low], 1)
    high = jnp.concatenate([re_high, im_high], 1)
    sums = []
    for k in range(2):
        first = dot(tables_of[2 * k][...], whole)
        second = dot(tables_of[2 * k + 1][...], high)
        sums.append(first[:, :128] + first[:, 128:256] + second[:, :128])
        sums.append(first[:, 256:384] + first[:, 384:] + second[:, 128:])
    return sums


def middle_kernel(place, arrived, *refs):
    echoes, given, out, sent = refs[:8], refs[8:15], refs[15], refs[16:24]
    held, resid, arrival = refs[24], refs[25], refs[33]
    copies = [
        pltpu.make_async_copy(source, target, arrival.at[k])
        for k, (source, target) in enumerate(zip(given, refs[26:33]))
    ]
    for copy in copies:
        copy.start()
    long, twist, mix, mix_back = refs[26:30], refs[30], refs[31], refs[32]
    for step in range(8):
        held[(place[0] + 8 - step) & 7] = echoes[step][...]
    parts = []
    for k in range(3):
        rows = []
        for odd in range(2):
            pieces = [held[2 * t1 + odd, k * 64 : (k + 1) * 64, :] for t1 in range(4)]
            rows += swap_groups(pieces, 32)
        parts.append(jnp.concatenate(rows, 0))
    for copy in copies:
        copy.wait()
    cos_re, cos_im, sin_re, sin_im = long_sums(
        arrived[pl.ds(0, 512, stride=2), :], arrived[pl.ds(1, 512, stride=2), :], long
    )
    re, im = cos_re - sin_im, sin_re + cos_im
    tr, ti = twist[0], twist[1]
    both = jnp.concatenate([re * tr - im * ti, re * ti + im * tr], 1)
    high, rest = split(both)
    field = dot(high, mix[...]) + dot(rest, mix[...])
    left = []
    for k in range(2):
        value = parts[2] * (parts[k] - field[:, k * 128 : (k + 1) * 128])
        left.append(value)
        for odd in range(2):
            pieces = [value[odd * 256 + q * 64 : odd * 256 + (q + 1) * 64] for q in range(4)]
            for t1, piece in enumerate(swap_groups(pieces, 32)):
                resid[2 * t1 + odd, k * 64 : (k + 1) * 64, :] = piece
    for step in range(8):
        sent[step][...] = resid[(place[0] + step) & 7]
    high, rest = split(jnp.concatenate(left, 1))
    mixed = dot(high, mix_back[...]) + dot(rest, mix_back[...])
    re, im = mixed[:, :128], mixed[:, 128:]
    cos_re, cos_im, sin_re, sin_im = long_sums(re * tr + im * ti, im * tr - re * ti, long)
    out[pl.ds(0, 512, stride=2), :] = cos_re + sin_im
    out[pl.ds(1, 512, stride=2), :] = cos_im - sin_re


def call(kernel, outs, *operands, near=0, apart=0, far=False, scratch=(), place=None, flops=0):
    single = not isinstance(outs, list)
    outs = [outs] if single else outs
    outs = [jax.ShapeDtypeStruct(o, f32) for o in outs]
    moved = sum(math.prod(o.shape) * o.dtype.itemsize for o in [*outs, *operands])
    spec = pl.BlockSpec(memory_space=pltpu.VMEM)
    in_specs = [spec] * (len(operands) - apart) + [pl.BlockSpec(memory_space=pl.ANY)] * apart
    operands = [
        pltpu.with_memory_space_constraint(o, pltpu.VMEM) if k < near else o
        for k, o in enumerate(operands)
    ]
    if place is not None:
        operands = [place, *operands]
        in_specs = [pl.BlockSpec(memory_space=pltpu.SMEM), *in_specs]
    out = pl.pallas_call(
        kernel,
        out_shape=outs if far else [pltpu.VMEM(o.shape, o.dtype) for o in outs],
        in_specs=in_specs,
        out_specs=[spec] * len(outs),
        scratch_shapes=[pltpu.VMEM(s, f32) if isinstance(s, tuple) else s for s in scratch],
        compiler_params=params,
        cost_estimate=pl.CostEstimate(flops=flops, bytes_accessed=moved, transcendentals=0),
    )(*operands)
    return out[0] if single else out


def exchange(value, axes):
    return lax.all_to_all(value, axes, split_axis=0, concat_axis=0, tiled=True)


def along_tx(pieces):
    moved = [pieces[0]]
    for step in range(1, 8):
        moved.append(lax.ppermute(pieces[step], "tx", [(i, (i + step) % 8) for i in range(8)]))
    return moved


def wave_numbers(indices, total):
    signed = jnp.where(indices < total // 2, indices, indices - total)
    return 2.0 * jnp.pi / total * signed.astype(f32)


def turns(wavenumber, tx, z, y):
    low = jnp.arange(8, dtype=jnp.int32) % 4
    sent = wave_numbers(tx * 256 + z * 16 + y * 4 + low, 2048)
    heard = wave_numbers(jnp.arange(2048, dtype=jnp.int32).reshape(16, 1, 1, 128), 2048)
    waves = jnp.repeat(wavenumber.reshape(4, 2), 4, axis=1)
    squared = waves * waves
    first = jnp.sqrt(jnp.maximum(squared - (sent * sent)[None, :], 0.0) + root_floor)
    second = jnp.sqrt(
        jnp.maximum(squared[None, :, :, None] - heard * heard, 0.0) + root_floor
    )
    phase = depth_step * (first[None, :, :, None] + second)
    return jnp.stack([jnp.cos(phase), jnp.sin(phase)])


def per_device(spectrum, measured, wavenumber, send_weight, hear_weight, aperture):
    table = tables()
    tx, z, y = lax.axis_index("tx"), lax.axis_index("rx"), lax.axis_index("freq")

    sent = call(send_kernel, (32, 2, 2, 8, 128), spectrum)
    arrived = exchange(sent.reshape(64, 16, 128), ("rx", "freq"))

    turn = turns(wavenumber, tx, z, y)
    place = tx.astype(jnp.int32).reshape(1)
    packed = call(
        pack_kernel,
        [(192, 128)] * 8,
        measured,
        send_weight.reshape(2, 128),
        hear_weight.reshape(1, 128),
        aperture,
        scratch=[(8, 192, 128)],
        place=place,
    )
    echoes = along_tx(packed)
    early = echoes[:early_echoes]
    pairs = call(
        pair_kernel,
        (1024, 128),
        arrived.reshape(16, 4, 2, 8, 128),
        turn,
        table["twist_heard"],
        *table["lanes"],
        *early,
        near=5,
        apart=len(early),
        flops=10**9,
    )
    columns = exchange(pairs.reshape(512, 2, 128), ("tx", "rx", "freq")).reshape(1024, 128)
    given = [*table["long"], table["twist_sent"], table["mix"], table["mix_back"]]
    given = [pltpu.with_memory_space_constraint(jnp.asarray(t), pltpu.HBM) for t in given]
    back, *resid = call(
        middle_kernel,
        [(1024, 128)] + [(128, 128)] * 8,
        columns,
        *echoes,
        *given,
        near=9,
        apart=7,
        scratch=[(8, 192, 128), (8, 128, 128)]
        + [pltpu.VMEM(t.shape, t.dtype) for t in given]
        + [pltpu.SemaphoreType.DMA((7,))],
        place=place,
        flops=3 * 10**9,
    )
    rows = exchange(back.reshape(512, 2, 128), ("tx", "rx", "freq")).reshape(1024, 128)
    pieces = along_tx(resid)
    residual = call(
        unpack_kernel,
        (2, 2, 256, 128),
        *pieces,
        near=8,
        far=True,
        scratch=[(8, 128, 128)],
        place=place,
    )
    early = pieces[:early_pieces]
    gradient = call(
        gradient_kernel,
        (16, 4, 2, 8, 128),
        rows,
        turn,
        table["twist_heard"],
        *table["lanes"],
        *early,
        near=5,
        apart=len(early),
        scratch=[(4, 16, 2, 8, 128)],
        flops=10**9,
    )
    gathered = exchange(gradient.reshape(64, 16, 128), ("rx", "freq"))
    updated = call(
        update_kernel,
        (2, 2, 256, 128),
        gathered.reshape(32, 2, 2, 8, 128),
        spectrum,
        near=2,
        far=True,
    )
    return updated, residual


def solution(mesh):
    placed = (
        P(None, "freq", "tx", "rx"),
        P(None, "freq", "tx", "rx"),
        P(),
        P("tx"),
        P("rx"),
        P("tx", "rx"),
    )
    return jax.shard_map(
        per_device,
        mesh=mesh,
        in_specs=placed,
        out_specs=(P(None, "freq", "tx", "rx"), P(None, "freq", "tx", "rx")),
        check_vma=False,
    )
```

```python
import functools
import math

import jax
import jax.numpy as jnp
import ml_dtypes
import numpy as np
from jax import lax
from jax.experimental import pallas as pl
from jax.experimental.pallas import tpu as pltpu
from jax.sharding import PartitionSpec as P

depth_step = 2.0
step_size = 0.125
root_floor = 0.25
early_echoes = 4
early_pieces = 5
bf16 = jnp.bfloat16
f32 = jnp.float32
nt_form = (((1,), (1,)), ((), ()))
params = pltpu.CompilerParams(vmem_limit_bytes=24 * 1024 * 1024)


def halves(table):
    high = table.astype(np.float32).astype(ml_dtypes.bfloat16)
    low = (table - high.astype(np.float64)).astype(np.float32).astype(ml_dtypes.bfloat16)
    return high, low


def angles(left, right, total):
    return 2.0 * np.pi / total * ((left[:, None] * right[None, :]) % total)


@functools.cache
def tables():
    index = np.arange(128)
    order = index.reshape(16, 8).T.reshape(-1)
    theta = angles(order, index, 128)
    scale = 1.0 / math.sqrt(2048.0)
    cosine, sine = np.cos(theta) * scale, np.sin(theta) * scale
    lanes = np.block([[cosine, -sine], [sine, cosine]])
    theta = angles(np.arange(16), index, 2048)
    twist_heard = np.stack([np.cos(theta), np.sin(theta)])
    twist_heard = np.broadcast_to(twist_heard[:, :, None, :], (2, 16, 8, 128)).astype(np.float32)
    index = np.arange(256)
    theta = angles(index, index, 256)
    long = halves(np.cos(theta) * scale) + halves(np.sin(theta) * scale)
    low_of_lane = np.arange(128) % 4
    theta = angles(index, low_of_lane, 2048)
    twist_sent = np.stack([np.cos(theta), np.sin(theta)]).astype(np.float32)
    mix = np.zeros((2, 16, 2, 4, 2, 4, 2, 16))
    quarter = ((1, 0), (0, 1), (-1, 0), (0, -1))
    for r0 in range(16):
        for f0 in range(2):
            for mi in range(4):
                for t1 in range(4):
                    c, s = quarter[mi * t1 % 4]
                    mix[0, r0, f0, mi, 0, t1, f0, r0] = c
                    mix[1, r0, f0, mi, 0, t1, f0, r0] = -s
                    mix[0, r0, f0, mi, 1, t1, f0, r0] = s
                    mix[1, r0, f0, mi, 1, t1, f0, r0] = c
    mix = mix.reshape(256, 256).astype(ml_dtypes.bfloat16)
    return dict(
        lanes=halves(lanes),
        twist_heard=twist_heard,
        long=long,
        twist_sent=twist_sent,
        mix=mix,
    )


def split(value):
    high = value.astype(bf16)
    return high, (value - high.astype(f32)).astype(bf16)


def dot(left, right):
    return jnp.dot(left, right, preferred_element_type=f32)


def swap_groups(arrays, width):
    arrays = list(arrays)
    group = lax.broadcasted_iota(jnp.int32, arrays[0].shape, 1) // width
    bit = 1
    while bit < len(arrays):
        high = (group & bit) != 0
        for i in range(len(arrays)):
            if i & bit:
                continue
            a, b = arrays[i], arrays[i | bit]
            arrays[i] = jnp.where(high, pltpu.roll(b, bit * width, 1), a)
            arrays[i | bit] = jnp.where(high, b, pltpu.roll(a, 128 - bit * width, 1))
        bit *= 2
    return arrays


def times(value, c, s):
    re, im = value
    if (c, s) == (1, 0):
        return value
    if (c, s) == (0, 1):
        return -im, re
    if (c, s) == (0, -1):
        return im, -re
    if (c, s) == (-1, 0):
        return -re, -im
    return re * c - im * s, re * s + im * c


def sixteen(values, sign):
    count = len(values)
    if count == 1:
        return values
    even = sixteen(values[0::2], sign)
    odd = sixteen(values[1::2], sign)
    first, second = [], []
    for k in range(count // 2):
        if 4 * k == 0:
            turn = (1, 0)
        elif 4 * k == count:
            turn = (0, sign)
        else:
            angle = 2.0 * math.pi * k / count
            turn = (math.cos(angle), sign * math.sin(angle))
        a, b = even[k], times(odd[k], *turn)
        first.append((a[0] + b[0], a[1] + b[1]))
        second.append((a[0] - b[0], a[1] - b[1]))
    return first + second


def send_kernel(spectrum, out):
    for c in range(2):
        a = spectrum[c, 0].reshape(32, 8, 128)
        b = spectrum[c, 1].reshape(32, 8, 128)
        low = lax.broadcasted_iota(jnp.int32, a.shape, 1) < 4
        out[:, 0, c] = jnp.where(low, a, pltpu.roll(b, 4, 1))
        out[:, 1, c] = jnp.where(low, pltpu.roll(a, 4, 1), b)


def update_kernel(arrived, spectrum, out):
    for c in range(2):
        a = arrived[:, 0, c]
        b = arrived[:, 1, c]
        low = lax.broadcasted_iota(jnp.int32, a.shape, 1) < 4
        first = jnp.where(low, a, pltpu.roll(b, 4, 1)).reshape(256, 128)
        second = jnp.where(low, pltpu.roll(a, 4, 1), b).reshape(256, 128)
        out[c, 0] = spectrum[c, 0] + step_size * first
        out[c, 1] = spectrum[c, 1] + step_size * second


def pack_kernel(place, measured, send, hear, gate, *refs):
    *outs, held = refs
    tile = lax.broadcasted_iota(jnp.int32, (256, 16), 0) // 16
    down = (tile == lax.broadcasted_iota(jnp.int32, (256, 16), 1)).astype(bf16)
    tile = lax.broadcasted_iota(jnp.int32, (8, 128), 1) // 16
    along = (tile == lax.broadcasted_iota(jnp.int32, (8, 128), 0)).astype(bf16)
    live = dot(dot(down, gate[...].astype(f32).astype(bf16)).astype(bf16), along)
    columns = [jnp.broadcast_to(send[k : k + 1, :], (128, 128)).T for k in range(2)]
    weights = jnp.concatenate(columns, 0) * hear[...] * live
    for k in range(3):
        pieces = []
        for q in range(4):
            for f0 in range(2):
                rows = slice(q * 64, (q + 1) * 64)
                pieces.append(measured[k, f0, rows, :] if k < 2 else weights[rows])
        for d, piece in enumerate(swap_groups(pieces, 16)):
            held[d, k * 64 : (k + 1) * 64, :] = piece
    for step in range(8):
        outs[step][...] = held[(place[0] + step) & 7]


def unpack_kernel(place, *refs):
    *arrived, out, held = refs
    for step in range(8):
        held[(place[0] + 8 - step) & 7] = arrived[step][...]
    for k in range(2):
        pieces = [held[d, k * 64 : (k + 1) * 64, :] for d in range(8)]
        for g, piece in enumerate(swap_groups(pieces, 16)):
            out[k, g % 2, pl.ds(g // 2 * 64, 64), :] = piece


def pair_kernel(arrived, turn, twist, table_high, table_low, *refs):
    out = refs[-1]
    low = lax.broadcasted_iota(jnp.int32, (8, 128), 0) < 4
    for y in range(4):
        points = []
        for z in range(16):
            wr, wi = turn[0, z, y], turn[1, z, y]
            pr = pi = None
            for layer in range(7, -1, -1):
                re, im = arrived[z, layer // 2, 0], arrived[z, layer // 2, 1]
                if layer % 2:
                    re = jnp.where(low, pltpu.roll(re, 4, 0), re)
                    im = jnp.where(low, pltpu.roll(im, 4, 0), im)
                else:
                    re = jnp.where(low, re, pltpu.roll(re, 4, 0))
                    im = jnp.where(low, im, pltpu.roll(im, 4, 0))
                if pr is not None:
                    re, im = re + (pr * wr + pi * wi), im + (pi * wr - pr * wi)
                pr, pi = re, im
            points.append((pr * wr + pi * wi, pi * wr - pr * wi))
        points = sixteen(points, 1)
        res, ims = [], []
        for r0, (re, im) in enumerate(points):
            tr, ti = twist[0, r0], twist[1, r0]
            res.append(re * tr - im * ti)
            ims.append(re * ti + im * tr)
        both = jnp.concatenate([jnp.concatenate(res, 0), jnp.concatenate(ims, 0)], 1)
        high, rest = split(both)
        stacked = jnp.concatenate([high, rest], 0)
        first = lax.dot_general(table_high[...], stacked, nt_form, preferred_element_type=f32)
        second = lax.dot_general(table_low[...], high, nt_form, preferred_element_type=f32)
        done = first[:, :128] + first[:, 128:] + second
        for c in range(2):
            out[pl.ds(y * 2 + c, 128, stride=8), :] = done[c * 128 : (c + 1) * 128]


def gradient_kernel(arrived, turn, twist, table_high, table_low, *refs):
    out, points = refs[-2:]
    for y in range(4):
        re = arrived[pl.ds(y * 2, 128, stride=8), :]
        im = arrived[pl.ds(y * 2 + 1, 128, stride=8), :]
        both = jnp.concatenate([re.T, im.T], 1)
        high, rest = split(both)
        first = dot(jnp.concatenate([high, rest], 0), table_high[...])
        done = first[:128] + first[128:] + dot(high, table_low[...])
        values = []
        for r0 in range(16):
            re = done[r0 * 8 : (r0 + 1) * 8, :128]
            im = done[r0 * 8 : (r0 + 1) * 8, 128:]
            tr, ti = twist[0, r0], twist[1, r0]
            values.append((re * tr + im * ti, im * tr - re * ti))
        for z, (re, im) in enumerate(sixteen(values, -1)):
            points[y, z, 0] = re
            points[y, z, 1] = im
    low = lax.broadcasted_iota(jnp.int32, (8, 128), 0) < 4
    for z in range(16):
        sums = [None] * 8
        for y in range(4):
            wr, wi = turn[0, z, y], turn[1, z, y]
            re, im = points[y, z, 0], points[y, z, 1]
            for layer in range(8):
                re, im = re * wr - im * wi, im * wr + re * wi
                if sums[layer] is None:
                    sums[layer] = (re, im)
                else:
                    sums[layer] = (sums[layer][0] + re, sums[layer][1] + im)
        for y in range(4):
            for c in range(2):
                a, b = sums[2 * y][c], sums[2 * y + 1][c]
                x = jnp.where(low, a, pltpu.roll(b, 4, 0))
                w = jnp.where(low, pltpu.roll(a, 4, 0), b)
                out[z, y, c] = x + w


def half_sums(pairs, tables_of):
    columns, highs = [], []
    for pair in pairs:
        for value in pair:
            high, rest = split(value)
            columns += [high, rest]
            highs.append(high)
    columns, highs = jnp.concatenate(columns, 1), jnp.concatenate(highs, 1)
    sums = []
    for k in range(2):
        first = dot(tables_of[2 * k][...], columns)
        second = dot(tables_of[2 * k + 1][...], highs)
        sums.append(
            [
                first[:, 256 * j : 256 * j + 128]
                + first[:, 256 * j + 128 : 256 * j + 256]
                + second[:, 128 * j : 128 * j + 128]
                for j in range(4)
            ]
        )
    cosine, sine = sums
    return [(*cosine[2 * p : 2 * p + 2], *sine[2 * p : 2 * p + 2]) for p in range(2)]


def turned(value, by):
    return value[0] * by[0] - value[1] * by[1], value[0] * by[1] + value[1] * by[0]


def turned_back(value, by):
    return value[0] * by[0] + value[1] * by[1], value[1] * by[0] - value[0] * by[1]


def sent_twists(twist):
    first = twist[0], twist[1]
    quarter = [jnp.broadcast_to(part[:, 2:3], part.shape) for part in first]
    low = lax.broadcasted_iota(jnp.int32, first[0].shape, 1) & 3
    half = math.sqrt(0.5)
    eighth = (
        jnp.where(low == 0, 1.0, jnp.where(low == 1, half, jnp.where(low == 2, 0.0, -half))),
        jnp.where(low == 0, 0.0, jnp.where(low == 2, 1.0, half)),
    )
    second = turned(first, eighth)
    whole = [jnp.concatenate([a, b], 0) for a, b in zip(first, second)]
    return whole, turned(quarter, quarter)


def middle_kernel(place, arrived, *refs):
    echoes, given, out, sent = refs[:8], refs[8:14], refs[14], refs[15:23]
    held, resid = refs[23:]
    for step in range(8):
        held[(place[0] + 8 - step) & 7] = echoes[step][...]
    parts = []
    for k in range(3):
        rows = []
        for odd in range(2):
            pieces = [held[2 * t1 + odd, k * 64 : (k + 1) * 64, :] for t1 in range(4)]
            rows += swap_groups(pieces, 32)
        parts.append(jnp.concatenate(rows, 0))
    long, twist, mix = given[:4], given[4], given[5][...]
    both_twists, odd_twist = sent_twists(twist)
    pairs = [
        tuple(arrived[pl.ds(2 * p + c, 256, stride=4), :] for c in range(2)) for p in range(2)
    ]
    even, odd = [
        (cos_re - sin_im, sin_re + cos_im)
        for cos_re, cos_im, sin_re, sin_im in half_sums(pairs, long)
    ]
    odd = turned(odd, odd_twist)
    value = [jnp.concatenate([a + b, a - b], 0) for a, b in zip(even, odd)]
    both = jnp.concatenate(turned(value, both_twists), 1)
    high, rest = split(both)
    field = dot(high, mix) + dot(rest, mix)
    left = []
    for k in range(2):
        value = parts[2] * (parts[k] - field[:, k * 128 : (k + 1) * 128])
        left.append(value)
        for odd in range(2):
            pieces = [value[odd * 256 + q * 64 : odd * 256 + (q + 1) * 64] for q in range(4)]
            for t1, piece in enumerate(swap_groups(pieces, 32)):
                resid[2 * t1 + odd, k * 64 : (k + 1) * 64, :] = piece
    for step in range(8):
        sent[step][...] = resid[(place[0] + step) & 7]
    mixed = sum(
        lax.dot_general(half, mix, nt_form, preferred_element_type=f32)
        for half in split(jnp.concatenate(left, 1))
    )
    value = turned_back((mixed[:, :128], mixed[:, 128:]), both_twists)
    even = [part[:256] + part[256:] for part in value]
    odd = turned_back([part[:256] - part[256:] for part in value], odd_twist)
    for p, sums in enumerate(half_sums([even, odd], long)):
        cos_re, cos_im, sin_re, sin_im = sums
        out[pl.ds(2 * p, 256, stride=4), :] = cos_re + sin_im
        out[pl.ds(2 * p + 1, 256, stride=4), :] = cos_im - sin_re


def call(kernel, outs, *operands, near=0, apart=0, far=False, scratch=(), place=None, flops=0):
    single = not isinstance(outs, list)
    outs = [outs] if single else outs
    outs = [jax.ShapeDtypeStruct(o, f32) for o in outs]
    moved = sum(math.prod(o.shape) * o.dtype.itemsize for o in [*outs, *operands])
    spec = pl.BlockSpec(memory_space=pltpu.VMEM)
    in_specs = [spec] * (len(operands) - apart) + [pl.BlockSpec(memory_space=pl.ANY)] * apart
    operands = [
        pltpu.with_memory_space_constraint(o, pltpu.VMEM) if k < near else o
        for k, o in enumerate(operands)
    ]
    if place is not None:
        operands = [place, *operands]
        in_specs = [pl.BlockSpec(memory_space=pltpu.SMEM), *in_specs]
    out = pl.pallas_call(
        kernel,
        out_shape=outs if far else [pltpu.VMEM(o.shape, o.dtype) for o in outs],
        in_specs=in_specs,
        out_specs=[spec] * len(outs),
        scratch_shapes=[pltpu.VMEM(s, f32) if isinstance(s, tuple) else s for s in scratch],
        compiler_params=params,
        cost_estimate=pl.CostEstimate(flops=flops, bytes_accessed=moved, transcendentals=0),
    )(*operands)
    return out[0] if single else out


def exchange(value, axes):
    return lax.all_to_all(value, axes, split_axis=0, concat_axis=0, tiled=True)


def along_tx(pieces):
    moved = [pieces[0]]
    for step in range(1, 8):
        moved.append(lax.ppermute(pieces[step], "tx", [(i, (i + step) % 8) for i in range(8)]))
    return moved


def wave_numbers(indices, total):
    signed = jnp.where(indices < total // 2, indices, indices - total)
    return 2.0 * jnp.pi / total * signed.astype(f32)


def turns(wavenumber, tx, z, y):
    low = jnp.arange(8, dtype=jnp.int32) % 4
    sent = wave_numbers(tx * 256 + z * 16 + y * 4 + low, 2048)
    heard = wave_numbers(jnp.arange(2048, dtype=jnp.int32).reshape(16, 1, 1, 128), 2048)
    waves = jnp.repeat(wavenumber.reshape(4, 2), 4, axis=1)
    squared = waves * waves
    first = jnp.sqrt(jnp.maximum(squared - (sent * sent)[None, :], 0.0) + root_floor)
    second = jnp.sqrt(
        jnp.maximum(squared[None, :, :, None] - heard * heard, 0.0) + root_floor
    )
    phase = depth_step * (first[None, :, :, None] + second)
    return jnp.stack([jnp.cos(phase), jnp.sin(phase)])


def per_device(spectrum, measured, wavenumber, send_weight, hear_weight, aperture):
    table = tables()
    tx, z, y = lax.axis_index("tx"), lax.axis_index("rx"), lax.axis_index("freq")

    sent = call(send_kernel, (32, 2, 2, 8, 128), spectrum)
    arrived = exchange(sent.reshape(64, 16, 128), ("rx", "freq"))

    turn = turns(wavenumber, tx, z, y)
    place = tx.astype(jnp.int32).reshape(1)
    packed = call(
        pack_kernel,
        [(192, 128)] * 8,
        measured,
        send_weight.reshape(2, 128),
        hear_weight.reshape(1, 128),
        aperture,
        scratch=[(8, 192, 128)],
        place=place,
    )
    echoes = along_tx(packed)
    early = echoes[:early_echoes]
    pairs = call(
        pair_kernel,
        (1024, 128),
        arrived.reshape(16, 4, 2, 8, 128),
        turn,
        table["twist_heard"],
        *table["lanes"],
        *early,
        near=5,
        apart=len(early),
        flops=10**9,
    )
    columns = exchange(pairs.reshape(512, 2, 128), ("tx", "rx", "freq")).reshape(1024, 128)
    given = [*table["long"], table["twist_sent"], table["mix"]]
    back, *resid = call(
        middle_kernel,
        [(1024, 128)] + [(128, 128)] * 8,
        columns,
        *echoes,
        *given,
        near=15,
        scratch=[(8, 192, 128), (8, 128, 128)],
        place=place,
        flops=3 * 10**9,
    )
    rows = exchange(back.reshape(512, 2, 128), ("tx", "rx", "freq")).reshape(1024, 128)
    pieces = along_tx(resid)
    residual = call(
        unpack_kernel,
        (2, 2, 256, 128),
        *pieces,
        near=8,
        far=True,
        scratch=[(8, 128, 128)],
        place=place,
    )
    early = pieces[:early_pieces]
    gradient = call(
        gradient_kernel,
        (16, 4, 2, 8, 128),
        rows,
        turn,
        table["twist_heard"],
        *table["lanes"],
        *early,
        near=5,
        apart=len(early),
        scratch=[(4, 16, 2, 8, 128)],
        flops=10**9,
    )
    gathered = exchange(gradient.reshape(64, 16, 128), ("rx", "freq"))
    updated = call(
        update_kernel,
        (2, 2, 256, 128),
        gathered.reshape(32, 2, 2, 8, 128),
        spectrum,
        near=2,
        far=True,
    )
    return updated, residual


def solution(mesh):
    placed = (
        P(None, "freq", "tx", "rx"),
        P(None, "freq", "tx", "rx"),
        P(),
        P("tx"),
        P("rx"),
        P("tx", "rx"),
    )
    return jax.shard_map(
        per_device,
        mesh=mesh,
        in_specs=placed,
        out_specs=(P(None, "freq", "tx", "rx"), P(None, "freq", "tx", "rx")),
        check_vma=False,
    )
```

```python
import functools
import math

import jax
import jax.numpy as jnp
import ml_dtypes
import numpy as np
from jax import lax
from jax.experimental import pallas as pl
from jax.experimental.pallas import tpu as pltpu
from jax.sharding import PartitionSpec as P

depth_step = 2.0
step_size = 0.125
root_floor = 0.25
early_echoes = 4
early_pieces = 5
bf16 = jnp.bfloat16
f32 = jnp.float32
nt_form = (((1,), (1,)), ((), ()))
params = pltpu.CompilerParams(vmem_limit_bytes=24 * 1024 * 1024)


def halves(table):
    high = table.astype(np.float32).astype(ml_dtypes.bfloat16)
    low = (table - high.astype(np.float64)).astype(np.float32).astype(ml_dtypes.bfloat16)
    return high, low


def angles(left, right, total):
    return 2.0 * np.pi / total * ((left[:, None] * right[None, :]) % total)


@functools.cache
def tables():
    index = np.arange(128)
    order = index.reshape(16, 8).T.reshape(-1)
    theta = angles(order, index, 128)
    scale = 1.0 / math.sqrt(2048.0)
    cosine, sine = np.cos(theta) * scale, np.sin(theta) * scale
    lanes = np.block([[cosine, -sine], [sine, cosine]])
    theta = angles(np.arange(16), index, 2048)
    twist_heard = np.stack([np.cos(theta), np.sin(theta)])
    twist_heard = np.broadcast_to(twist_heard[:, :, None, :], (2, 16, 8, 128)).astype(np.float32)
    index = np.arange(256)
    theta = angles(index, index, 256)
    long = halves(np.cos(theta) * scale) + halves(np.sin(theta) * scale)
    low_of_lane = np.arange(128) % 4
    theta = angles(index, low_of_lane, 2048)
    twist_sent = np.stack([np.cos(theta), np.sin(theta)]).astype(np.float32)
    mix = np.zeros((2, 16, 2, 4, 2, 4, 2, 16))
    quarter = ((1, 0), (0, 1), (-1, 0), (0, -1))
    for r0 in range(16):
        for f0 in range(2):
            for mi in range(4):
                for t1 in range(4):
                    c, s = quarter[mi * t1 % 4]
                    mix[0, r0, f0, mi, 0, t1, f0, r0] = c
                    mix[1, r0, f0, mi, 0, t1, f0, r0] = -s
                    mix[0, r0, f0, mi, 1, t1, f0, r0] = s
                    mix[1, r0, f0, mi, 1, t1, f0, r0] = c
    mix = mix.reshape(256, 256).astype(ml_dtypes.bfloat16)
    return dict(
        lanes=halves(lanes),
        twist_heard=twist_heard,
        long=long,
        twist_sent=twist_sent,
        mix=mix,
    )


def split(value):
    high = value.astype(bf16)
    return high, (value - high.astype(f32)).astype(bf16)


def dot(left, right):
    return jnp.dot(left, right, preferred_element_type=f32)


def swap_groups(arrays, width):
    arrays = list(arrays)
    group = lax.broadcasted_iota(jnp.int32, arrays[0].shape, 1) // width
    bit = 1
    while bit < len(arrays):
        high = (group & bit) != 0
        for i in range(len(arrays)):
            if i & bit:
                continue
            a, b = arrays[i], arrays[i | bit]
            arrays[i] = jnp.where(high, pltpu.roll(b, bit * width, 1), a)
            arrays[i | bit] = jnp.where(high, b, pltpu.roll(a, 128 - bit * width, 1))
        bit *= 2
    return arrays


def times(value, c, s):
    re, im = value
    if (c, s) == (1, 0):
        return value
    if (c, s) == (0, 1):
        return -im, re
    if (c, s) == (0, -1):
        return im, -re
    if (c, s) == (-1, 0):
        return -re, -im
    return re * c - im * s, re * s + im * c


def sixteen(values, sign):
    count = len(values)
    if count == 1:
        return values
    even = sixteen(values[0::2], sign)
    odd = sixteen(values[1::2], sign)
    first, second = [], []
    for k in range(count // 2):
        if 4 * k == 0:
            turn = (1, 0)
        elif 4 * k == count:
            turn = (0, sign)
        else:
            angle = 2.0 * math.pi * k / count
            turn = (math.cos(angle), sign * math.sin(angle))
        a, b = even[k], times(odd[k], *turn)
        first.append((a[0] + b[0], a[1] + b[1]))
        second.append((a[0] - b[0], a[1] - b[1]))
    return first + second


def send_kernel(spectrum, out, held, arrival):
    parts = [(c, h) for c in range(2) for h in range(2)]
    copies = []
    for k, (c, h) in enumerate(parts):
        rows = pl.ds(h * 128, 128)
        copies.append(
            pltpu.make_async_copy(spectrum.at[c, :, rows], held.at[c, :, rows], arrival.at[k])
        )
    for copy in copies:
        copy.start()
    for copy, (c, h) in zip(copies, parts):
        copy.wait()
        a = held[c, 0, h * 128 : (h + 1) * 128].reshape(16, 8, 128)
        b = held[c, 1, h * 128 : (h + 1) * 128].reshape(16, 8, 128)
        low = lax.broadcasted_iota(jnp.int32, a.shape, 1) < 4
        out[16 * h : 16 * h + 16, 0, c] = jnp.where(low, a, pltpu.roll(b, 4, 1))
        out[16 * h : 16 * h + 16, 1, c] = jnp.where(low, pltpu.roll(a, 4, 1), b)


def update_kernel(arrived, spectrum, out):
    for c in range(2):
        a = arrived[:, 0, c]
        b = arrived[:, 1, c]
        low = lax.broadcasted_iota(jnp.int32, a.shape, 1) < 4
        first = jnp.where(low, a, pltpu.roll(b, 4, 1)).reshape(256, 128)
        second = jnp.where(low, pltpu.roll(a, 4, 1), b).reshape(256, 128)
        out[c, 0] = spectrum[c, 0] + step_size * first
        out[c, 1] = spectrum[c, 1] + step_size * second


def pack_kernel(place, measured, send, hear, gate, *refs):
    *outs, held = refs
    tile = lax.broadcasted_iota(jnp.int32, (256, 16), 0) // 16
    down = (tile == lax.broadcasted_iota(jnp.int32, (256, 16), 1)).astype(bf16)
    tile = lax.broadcasted_iota(jnp.int32, (8, 128), 1) // 16
    along = (tile == lax.broadcasted_iota(jnp.int32, (8, 128), 0)).astype(bf16)
    live = dot(dot(down, gate[...].astype(f32).astype(bf16)).astype(bf16), along)
    columns = [jnp.broadcast_to(send[k : k + 1, :], (128, 128)).T for k in range(2)]
    weights = jnp.concatenate(columns, 0) * hear[...] * live
    for k in range(3):
        pieces = []
        for q in range(4):
            for f0 in range(2):
                rows = slice(q * 64, (q + 1) * 64)
                pieces.append(measured[k, f0, rows, :] if k < 2 else weights[rows])
        for d, piece in enumerate(swap_groups(pieces, 16)):
            held[d, k * 64 : (k + 1) * 64, :] = piece
    for step in range(8):
        outs[step][...] = held[(place[0] + step) & 7]


def unpack_kernel(place, *refs):
    *arrived, out, held = refs
    for step in range(8):
        held[(place[0] + 8 - step) & 7] = arrived[step][...]
    for k in range(2):
        pieces = [held[d, k * 64 : (k + 1) * 64, :] for d in range(8)]
        for g, piece in enumerate(swap_groups(pieces, 16)):
            out[k, g % 2, pl.ds(g // 2 * 64, 64), :] = piece


def pair_kernel(arrived, turn, twist, table_high, table_low, *refs):
    out = refs[-1]
    low = lax.broadcasted_iota(jnp.int32, (8, 128), 0) < 4
    for y in range(4):
        points = []
        for z in range(16):
            wr, wi = turn[0, z, y], turn[1, z, y]
            pr = pi = None
            for layer in range(7, -1, -1):
                re, im = arrived[z, layer // 2, 0], arrived[z, layer // 2, 1]
                if layer % 2:
                    re = jnp.where(low, pltpu.roll(re, 4, 0), re)
                    im = jnp.where(low, pltpu.roll(im, 4, 0), im)
                else:
                    re = jnp.where(low, re, pltpu.roll(re, 4, 0))
                    im = jnp.where(low, im, pltpu.roll(im, 4, 0))
                if pr is not None:
                    re, im = re + (pr * wr + pi * wi), im + (pi * wr - pr * wi)
                pr, pi = re, im
            points.append((pr * wr + pi * wi, pi * wr - pr * wi))
        points = sixteen(points, 1)
        res, ims = [], []
        for r0, (re, im) in enumerate(points):
            tr, ti = twist[0, r0], twist[1, r0]
            res.append(re * tr - im * ti)
            ims.append(re * ti + im * tr)
        both = jnp.concatenate([jnp.concatenate(res, 0), jnp.concatenate(ims, 0)], 1)
        high, rest = split(both)
        stacked = jnp.concatenate([high, rest], 0)
        first = lax.dot_general(table_high[...], stacked, nt_form, preferred_element_type=f32)
        second = lax.dot_general(table_low[...], high, nt_form, preferred_element_type=f32)
        done = first[:, :128] + first[:, 128:] + second
        for c in range(2):
            out[pl.ds(y * 2 + c, 128, stride=8), :] = done[c * 128 : (c + 1) * 128]


def gradient_kernel(arrived, turn, twist, table_high, table_low, *refs):
    out, points = refs[-2:]
    for y in range(4):
        re = arrived[pl.ds(y * 2, 128, stride=8), :]
        im = arrived[pl.ds(y * 2 + 1, 128, stride=8), :]
        both = jnp.concatenate([re.T, im.T], 1)
        high, rest = split(both)
        first = dot(jnp.concatenate([high, rest], 0), table_high[...])
        done = first[:128] + first[128:] + dot(high, table_low[...])
        values = []
        for r0 in range(16):
            re = done[r0 * 8 : (r0 + 1) * 8, :128]
            im = done[r0 * 8 : (r0 + 1) * 8, 128:]
            tr, ti = twist[0, r0], twist[1, r0]
            values.append((re * tr + im * ti, im * tr - re * ti))
        for z, (re, im) in enumerate(sixteen(values, -1)):
            points[y, z, 0] = re
            points[y, z, 1] = im
    low = lax.broadcasted_iota(jnp.int32, (8, 128), 0) < 4
    for z in range(16):
        sums = [None] * 8
        for y in range(4):
            wr, wi = turn[0, z, y], turn[1, z, y]
            re, im = points[y, z, 0], points[y, z, 1]
            for layer in range(8):
                re, im = re * wr - im * wi, im * wr + re * wi
                if sums[layer] is None:
                    sums[layer] = (re, im)
                else:
                    sums[layer] = (sums[layer][0] + re, sums[layer][1] + im)
        for y in range(4):
            for c in range(2):
                a, b = sums[2 * y][c], sums[2 * y + 1][c]
                x = jnp.where(low, a, pltpu.roll(b, 4, 0))
                w = jnp.where(low, pltpu.roll(a, 4, 0), b)
                out[z, y, c] = x + w


def half_sums(pairs, tables_of):
    columns, highs = [], []
    for pair in pairs:
        for value in pair:
            high, rest = split(value)
            columns += [high, rest]
            highs.append(high)
    columns, highs = jnp.concatenate(columns, 1), jnp.concatenate(highs, 1)
    sums = []
    for k in range(2):
        first = dot(tables_of[2 * k][...], columns)
        second = dot(tables_of[2 * k + 1][...], highs)
        sums.append(
            [
                first[:, 256 * j : 256 * j + 128]
                + first[:, 256 * j + 128 : 256 * j + 256]
                + second[:, 128 * j : 128 * j + 128]
                for j in range(4)
            ]
        )
    cosine, sine = sums
    return [(*cosine[2 * p : 2 * p + 2], *sine[2 * p : 2 * p + 2]) for p in range(2)]


def turned(value, by):
    return value[0] * by[0] - value[1] * by[1], value[0] * by[1] + value[1] * by[0]


def turned_back(value, by):
    return value[0] * by[0] + value[1] * by[1], value[1] * by[0] - value[0] * by[1]


def sent_twists(twist):
    first = twist[0], twist[1]
    quarter = [jnp.broadcast_to(part[:, 2:3], part.shape) for part in first]
    low = lax.broadcasted_iota(jnp.int32, first[0].shape, 1) & 3
    half = math.sqrt(0.5)
    eighth = (
        jnp.where(low == 0, 1.0, jnp.where(low == 1, half, jnp.where(low == 2, 0.0, -half))),
        jnp.where(low == 0, 0.0, jnp.where(low == 2, 1.0, half)),
    )
    second = turned(first, eighth)
    whole = [jnp.concatenate([a, b], 0) for a, b in zip(first, second)]
    return whole, turned(quarter, quarter)


def middle_kernel(place, arrived, *refs):
    echoes, given, out, sent = refs[:8], refs[8:14], refs[14], refs[15:23]
    held, resid, first, arrival = refs[23:]
    copy = pltpu.make_async_copy(given[5], first, arrival)
    copy.start()
    for step in range(8):
        held[(place[0] + 8 - step) & 7] = echoes[step][...]
    parts = []
    for k in range(3):
        rows = []
        for odd in range(2):
            pieces = [held[2 * t1 + odd, k * 64 : (k + 1) * 64, :] for t1 in range(4)]
            rows += swap_groups(pieces, 32)
        parts.append(jnp.concatenate(rows, 0))
    copy.wait()
    long, twist, mix = [first, *given[:3]], given[3], given[4][...]
    both_twists, odd_twist = sent_twists(twist)
    pairs = [
        tuple(arrived[pl.ds(2 * p + c, 256, stride=4), :] for c in range(2)) for p in range(2)
    ]
    even, odd = [
        (cos_re - sin_im, sin_re + cos_im)
        for cos_re, cos_im, sin_re, sin_im in half_sums(pairs, long)
    ]
    odd = turned(odd, odd_twist)
    value = [jnp.concatenate([a + b, a - b], 0) for a, b in zip(even, odd)]
    both = jnp.concatenate(turned(value, both_twists), 1)
    high, rest = split(both)
    field = dot(high, mix) + dot(rest, mix)
    left = []
    for k in range(2):
        value = parts[2] * (parts[k] - field[:, k * 128 : (k + 1) * 128])
        left.append(value)
        for odd in range(2):
            pieces = [value[odd * 256 + q * 64 : odd * 256 + (q + 1) * 64] for q in range(4)]
            for t1, piece in enumerate(swap_groups(pieces, 32)):
                resid[2 * t1 + odd, k * 64 : (k + 1) * 64, :] = piece
    for step in range(8):
        sent[step][...] = resid[(place[0] + step) & 7]
    mixed = sum(
        lax.dot_general(half, mix, nt_form, preferred_element_type=f32)
        for half in split(jnp.concatenate(left, 1))
    )
    value = turned_back((mixed[:, :128], mixed[:, 128:]), both_twists)
    even = [part[:256] + part[256:] for part in value]
    odd = turned_back([part[:256] - part[256:] for part in value], odd_twist)
    for p, sums in enumerate(half_sums([even, odd], long)):
        cos_re, cos_im, sin_re, sin_im = sums
        out[pl.ds(2 * p, 256, stride=4), :] = cos_re + sin_im
        out[pl.ds(2 * p + 1, 256, stride=4), :] = cos_im - sin_re


def call(kernel, outs, *operands, near=0, apart=0, far=False, scratch=(), place=None, flops=0):
    single = not isinstance(outs, list)
    outs = [outs] if single else outs
    outs = [jax.ShapeDtypeStruct(o, f32) for o in outs]
    moved = sum(math.prod(o.shape) * o.dtype.itemsize for o in [*outs, *operands])
    spec = pl.BlockSpec(memory_space=pltpu.VMEM)
    in_specs = [spec] * (len(operands) - apart) + [pl.BlockSpec(memory_space=pl.ANY)] * apart
    operands = [
        pltpu.with_memory_space_constraint(o, pltpu.VMEM) if k < near else o
        for k, o in enumerate(operands)
    ]
    if place is not None:
        operands = [place, *operands]
        in_specs = [pl.BlockSpec(memory_space=pltpu.SMEM), *in_specs]
    out = pl.pallas_call(
        kernel,
        out_shape=outs if far else [pltpu.VMEM(o.shape, o.dtype) for o in outs],
        in_specs=in_specs,
        out_specs=[spec] * len(outs),
        scratch_shapes=[pltpu.VMEM(s, f32) if isinstance(s, tuple) else s for s in scratch],
        compiler_params=params,
        cost_estimate=pl.CostEstimate(flops=flops, bytes_accessed=moved, transcendentals=0),
    )(*operands)
    return out[0] if single else out


def exchange(value, axes):
    return lax.all_to_all(value, axes, split_axis=0, concat_axis=0, tiled=True)


def along_tx(pieces):
    moved = [pieces[0]]
    for step in range(1, 8):
        moved.append(lax.ppermute(pieces[step], "tx", [(i, (i + step) % 8) for i in range(8)]))
    return moved


def wave_numbers(indices, total):
    signed = jnp.where(indices < total // 2, indices, indices - total)
    return 2.0 * jnp.pi / total * signed.astype(f32)


def turns(wavenumber, tx, z, y):
    low = jnp.arange(8, dtype=jnp.int32) % 4
    sent = wave_numbers(tx * 256 + z * 16 + y * 4 + low, 2048)
    heard = wave_numbers(jnp.arange(2048, dtype=jnp.int32).reshape(16, 1, 1, 128), 2048)
    waves = jnp.repeat(wavenumber.reshape(4, 2), 4, axis=1)
    squared = waves * waves
    first = jnp.sqrt(jnp.maximum(squared - (sent * sent)[None, :], 0.0) + root_floor)
    second = jnp.sqrt(
        jnp.maximum(squared[None, :, :, None] - heard * heard, 0.0) + root_floor
    )
    phase = depth_step * (first[None, :, :, None] + second)
    return jnp.stack([jnp.cos(phase), jnp.sin(phase)])


def per_device(spectrum, measured, wavenumber, send_weight, hear_weight, aperture):
    table = tables()
    tx, z, y = lax.axis_index("tx"), lax.axis_index("rx"), lax.axis_index("freq")

    sent = call(
        send_kernel,
        (32, 2, 2, 8, 128),
        pltpu.with_memory_space_constraint(spectrum, pltpu.HBM),
        apart=1,
        scratch=[(2, 2, 256, 128), pltpu.SemaphoreType.DMA((4,))],
    )
    arrived = exchange(sent.reshape(64, 16, 128), ("rx", "freq"))

    turn = turns(wavenumber, tx, z, y)
    place = tx.astype(jnp.int32).reshape(1)
    packed = call(
        pack_kernel,
        [(192, 128)] * 8,
        measured,
        send_weight.reshape(2, 128),
        hear_weight.reshape(1, 128),
        aperture,
        scratch=[(8, 192, 128)],
        place=place,
    )
    echoes = along_tx(packed)
    early = echoes[:early_echoes]
    pairs = call(
        pair_kernel,
        (1024, 128),
        arrived.reshape(16, 4, 2, 8, 128),
        turn,
        table["twist_heard"],
        *table["lanes"],
        *early,
        near=5,
        apart=len(early),
        flops=10**9,
    )
    columns = exchange(pairs.reshape(512, 2, 128), ("tx", "rx", "freq")).reshape(1024, 128)
    given = [*table["long"][1:], table["twist_sent"], table["mix"]]
    given.append(pltpu.with_memory_space_constraint(jnp.asarray(table["long"][0]), pltpu.HBM))
    back, *resid = call(
        middle_kernel,
        [(1024, 128)] + [(128, 128)] * 8,
        columns,
        *echoes,
        *given,
        near=14,
        apart=1,
        scratch=[
            (8, 192, 128),
            (8, 128, 128),
            pltpu.VMEM((256, 256), bf16),
            pltpu.SemaphoreType.DMA,
        ],
        place=place,
        flops=3 * 10**9,
    )
    rows = exchange(back.reshape(512, 2, 128), ("tx", "rx", "freq")).reshape(1024, 128)
    pieces = along_tx(resid)
    residual = call(
        unpack_kernel,
        (2, 2, 256, 128),
        *pieces,
        near=8,
        far=True,
        scratch=[(8, 128, 128)],
        place=place,
    )
    early = pieces[:early_pieces]
    gradient = call(
        gradient_kernel,
        (16, 4, 2, 8, 128),
        rows,
        turn,
        table["twist_heard"],
        *table["lanes"],
        *early,
        near=5,
        apart=len(early),
        scratch=[(4, 16, 2, 8, 128)],
        flops=10**9,
    )
    gathered = exchange(gradient.reshape(64, 16, 128), ("rx", "freq"))
    updated = call(
        update_kernel,
        (2, 2, 256, 128),
        gathered.reshape(32, 2, 2, 8, 128),
        spectrum,
        near=2,
        far=True,
    )
    return updated, residual


def solution(mesh):
    placed = (
        P(None, "freq", "tx", "rx"),
        P(None, "freq", "tx", "rx"),
        P(),
        P("tx"),
        P("rx"),
        P("tx", "rx"),
    )
    return jax.shard_map(
        per_device,
        mesh=mesh,
        in_specs=placed,
        out_specs=(P(None, "freq", "tx", "rx"), P(None, "freq", "tx", "rx")),
        check_vma=False,
    )
```

```python
import functools
import math

import jax
import jax.numpy as jnp
import ml_dtypes
import numpy as np
from jax import lax
from jax.experimental import pallas as pl
from jax.experimental.pallas import tpu as pltpu
from jax.sharding import PartitionSpec as P

depth_step = 2.0
step_size = 0.125
root_floor = 0.25
early_echoes = 4
early_pieces = 5
bf16 = jnp.bfloat16
f32 = jnp.float32
nt_form = (((1,), (1,)), ((), ()))
params = pltpu.CompilerParams(vmem_limit_bytes=24 * 1024 * 1024)


def halves(table):
    high = table.astype(np.float32).astype(ml_dtypes.bfloat16)
    low = (table - high.astype(np.float64)).astype(np.float32).astype(ml_dtypes.bfloat16)
    return high, low


def angles(left, right, total):
    return 2.0 * np.pi / total * ((left[:, None] * right[None, :]) % total)


@functools.cache
def tables():
    index = np.arange(128)
    order = index.reshape(16, 8).T.reshape(-1)
    theta = angles(order, index, 128)
    scale = 1.0 / math.sqrt(2048.0)
    cosine, sine = np.cos(theta) * scale, np.sin(theta) * scale
    lanes = np.block([[cosine, -sine], [sine, cosine]])
    theta = angles(np.arange(16), index, 2048)
    twist_heard = np.stack([np.cos(theta), np.sin(theta)])
    twist_heard = np.broadcast_to(twist_heard[:, :, None, :], (2, 16, 8, 128)).astype(np.float32)
    index = np.arange(256)
    theta = angles(index, index, 256)
    long = halves(np.cos(theta) * scale) + halves(np.sin(theta) * scale)
    low_of_lane = np.arange(128) % 4
    theta = angles(index, low_of_lane, 2048)
    twist_sent = np.stack([np.cos(theta), np.sin(theta)]).astype(np.float32)
    mix = np.zeros((2, 16, 2, 4, 2, 4, 2, 16))
    quarter = ((1, 0), (0, 1), (-1, 0), (0, -1))
    for r0 in range(16):
        for f0 in range(2):
            for mi in range(4):
                for t1 in range(4):
                    c, s = quarter[mi * t1 % 4]
                    mix[0, r0, f0, mi, 0, t1, f0, r0] = c
                    mix[1, r0, f0, mi, 0, t1, f0, r0] = -s
                    mix[0, r0, f0, mi, 1, t1, f0, r0] = s
                    mix[1, r0, f0, mi, 1, t1, f0, r0] = c
    mix = mix.reshape(256, 256).astype(ml_dtypes.bfloat16)
    return dict(
        lanes=halves(lanes),
        twist_heard=twist_heard,
        long=long,
        twist_sent=twist_sent,
        mix=mix,
    )


def split(value):
    high = value.astype(bf16)
    return high, (value - high.astype(f32)).astype(bf16)


def dot(left, right):
    return jnp.dot(left, right, preferred_element_type=f32)


def swap_groups(arrays, width):
    arrays = list(arrays)
    group = lax.broadcasted_iota(jnp.int32, arrays[0].shape, 1) // width
    bit = 1
    while bit < len(arrays):
        high = (group & bit) != 0
        for i in range(len(arrays)):
            if i & bit:
                continue
            a, b = arrays[i], arrays[i | bit]
            arrays[i] = jnp.where(high, pltpu.roll(b, bit * width, 1), a)
            arrays[i | bit] = jnp.where(high, b, pltpu.roll(a, 128 - bit * width, 1))
        bit *= 2
    return arrays


def times(value, c, s):
    re, im = value
    if (c, s) == (1, 0):
        return value
    if (c, s) == (0, 1):
        return -im, re
    if (c, s) == (0, -1):
        return im, -re
    if (c, s) == (-1, 0):
        return -re, -im
    return re * c - im * s, re * s + im * c


def sixteen(values, sign):
    count = len(values)
    if count == 1:
        return values
    even = sixteen(values[0::2], sign)
    odd = sixteen(values[1::2], sign)
    first, second = [], []
    for k in range(count // 2):
        if 4 * k == 0:
            turn = (1, 0)
        elif 4 * k == count:
            turn = (0, sign)
        else:
            angle = 2.0 * math.pi * k / count
            turn = (math.cos(angle), sign * math.sin(angle))
        a, b = even[k], times(odd[k], *turn)
        first.append((a[0] + b[0], a[1] + b[1]))
        second.append((a[0] - b[0], a[1] - b[1]))
    return first + second


def send_kernel(spectrum, out):
    for c in range(2):
        a = spectrum[c, 0].reshape(32, 8, 128)
        b = spectrum[c, 1].reshape(32, 8, 128)
        low = lax.broadcasted_iota(jnp.int32, a.shape, 1) < 4
        out[:, 0, c] = jnp.where(low, a, pltpu.roll(b, 4, 1))
        out[:, 1, c] = jnp.where(low, pltpu.roll(a, 4, 1), b)


def update_kernel(arrived, spectrum, out):
    for c in range(2):
        a = arrived[:, 0, c]
        b = arrived[:, 1, c]
        low = lax.broadcasted_iota(jnp.int32, a.shape, 1) < 4
        first = jnp.where(low, a, pltpu.roll(b, 4, 1)).reshape(256, 128)
        second = jnp.where(low, pltpu.roll(a, 4, 1), b).reshape(256, 128)
        out[c, 0] = spectrum[c, 0] + step_size * first
        out[c, 1] = spectrum[c, 1] + step_size * second


def pack_kernel(place, measured, send, hear, gate, *refs):
    *outs, held = refs
    tile = lax.broadcasted_iota(jnp.int32, (256, 16), 0) // 16
    down = (tile == lax.broadcasted_iota(jnp.int32, (256, 16), 1)).astype(bf16)
    tile = lax.broadcasted_iota(jnp.int32, (8, 128), 1) // 16
    along = (tile == lax.broadcasted_iota(jnp.int32, (8, 128), 0)).astype(bf16)
    live = dot(dot(down, gate[...].astype(f32).astype(bf16)).astype(bf16), along)
    columns = [jnp.broadcast_to(send[k : k + 1, :], (128, 128)).T for k in range(2)]
    weights = jnp.concatenate(columns, 0) * hear[...] * live
    for k in range(3):
        pieces = []
        for q in range(4):
            for f0 in range(2):
                rows = slice(q * 64, (q + 1) * 64)
                pieces.append(measured[k, f0, rows, :] if k < 2 else weights[rows])
        for d, piece in enumerate(swap_groups(pieces, 16)):
            held[d, k * 64 : (k + 1) * 64, :] = piece
    for step in range(8):
        outs[step][...] = held[(place[0] + step) & 7]


def unpack_kernel(place, *refs):
    *arrived, out, held = refs
    for step in range(8):
        held[(place[0] + 8 - step) & 7] = arrived[step][...]
    for k in range(2):
        pieces = [held[d, k * 64 : (k + 1) * 64, :] for d in range(8)]
        for g, piece in enumerate(swap_groups(pieces, 16)):
            out[k, g % 2, pl.ds(g // 2 * 64, 64), :] = piece


def pair_kernel(arrived, turn, twist, table_high, table_low, *refs):
    out = refs[-1]
    low = lax.broadcasted_iota(jnp.int32, (8, 128), 0) < 4
    for y in range(4):
        points = []
        for z in range(16):
            wr, wi = turn[0, z, y], turn[1, z, y]
            pr = pi = None
            for layer in range(7, -1, -1):
                re, im = arrived[z, layer // 2, 0], arrived[z, layer // 2, 1]
                if layer % 2:
                    re = jnp.where(low, pltpu.roll(re, 4, 0), re)
                    im = jnp.where(low, pltpu.roll(im, 4, 0), im)
                else:
                    re = jnp.where(low, re, pltpu.roll(re, 4, 0))
                    im = jnp.where(low, im, pltpu.roll(im, 4, 0))
                if pr is not None:
                    re, im = re + (pr * wr + pi * wi), im + (pi * wr - pr * wi)
                pr, pi = re, im
            points.append((pr * wr + pi * wi, pi * wr - pr * wi))
        points = sixteen(points, 1)
        res, ims = [], []
        for r0, (re, im) in enumerate(points):
            tr, ti = twist[0, r0], twist[1, r0]
            res.append(re * tr - im * ti)
            ims.append(re * ti + im * tr)
        both = jnp.concatenate([jnp.concatenate(res, 0), jnp.concatenate(ims, 0)], 1)
        high, rest = split(both)
        stacked = jnp.concatenate([high, rest], 0)
        first = lax.dot_general(table_high[...], stacked, nt_form, preferred_element_type=f32)
        second = lax.dot_general(table_low[...], high, nt_form, preferred_element_type=f32)
        done = first[:, :128] + first[:, 128:] + second
        for c in range(2):
            out[pl.ds(y * 2 + c, 128, stride=8), :] = done[c * 128 : (c + 1) * 128]


def gradient_kernel(arrived, turn, twist, table_high, table_low, *refs):
    out, points = refs[-2:]
    for y in range(4):
        re = arrived[pl.ds(y * 2, 128, stride=8), :]
        im = arrived[pl.ds(y * 2 + 1, 128, stride=8), :]
        both = jnp.concatenate([re.T, im.T], 1)
        high, rest = split(both)
        first = dot(jnp.concatenate([high, rest], 0), table_high[...])
        done = first[:128] + first[128:] + dot(high, table_low[...])
        values = []
        for r0 in range(16):
            re = done[r0 * 8 : (r0 + 1) * 8, :128]
            im = done[r0 * 8 : (r0 + 1) * 8, 128:]
            tr, ti = twist[0, r0], twist[1, r0]
            values.append((re * tr + im * ti, im * tr - re * ti))
        for z, (re, im) in enumerate(sixteen(values, -1)):
            points[y, z, 0] = re
            points[y, z, 1] = im
    low = lax.broadcasted_iota(jnp.int32, (8, 128), 0) < 4
    for z in range(16):
        sums = [None] * 8
        for y in range(4):
            wr, wi = turn[0, z, y], turn[1, z, y]
            re, im = points[y, z, 0], points[y, z, 1]
            for layer in range(8):
                re, im = re * wr - im * wi, im * wr + re * wi
                if sums[layer] is None:
                    sums[layer] = (re, im)
                else:
                    sums[layer] = (sums[layer][0] + re, sums[layer][1] + im)
        for y in range(4):
            for c in range(2):
                a, b = sums[2 * y][c], sums[2 * y + 1][c]
                x = jnp.where(low, a, pltpu.roll(b, 4, 0))
                w = jnp.where(low, pltpu.roll(a, 4, 0), b)
                out[z, y, c] = x + w


def half_sums(pairs, tables_of):
    columns, highs = [], []
    for pair in pairs:
        for value in pair:
            high, rest = split(value)
            columns += [high, rest]
            highs.append(high)
    columns, highs = jnp.concatenate(columns, 1), jnp.concatenate(highs, 1)
    sums = []
    for k in range(2):
        first = dot(tables_of[2 * k][...], columns)
        second = dot(tables_of[2 * k + 1][...], highs)
        sums.append(
            [
                first[:, 256 * j : 256 * j + 128]
                + first[:, 256 * j + 128 : 256 * j + 256]
                + second[:, 128 * j : 128 * j + 128]
                for j in range(4)
            ]
        )
    cosine, sine = sums
    return [(*cosine[2 * p : 2 * p + 2], *sine[2 * p : 2 * p + 2]) for p in range(2)]


def turned(value, by):
    return value[0] * by[0] - value[1] * by[1], value[0] * by[1] + value[1] * by[0]


def turned_back(value, by):
    return value[0] * by[0] + value[1] * by[1], value[1] * by[0] - value[0] * by[1]


def sent_twists(twist):
    first = twist[0], twist[1]
    quarter = [jnp.broadcast_to(part[:, 2:3], part.shape) for part in first]
    low = lax.broadcasted_iota(jnp.int32, first[0].shape, 1) & 3
    half = math.sqrt(0.5)
    eighth = (
        jnp.where(low == 0, 1.0, jnp.where(low == 1, half, jnp.where(low == 2, 0.0, -half))),
        jnp.where(low == 0, 0.0, jnp.where(low == 2, 1.0, half)),
    )
    second = turned(first, eighth)
    whole = [jnp.concatenate([a, b], 0) for a, b in zip(first, second)]
    return whole, turned(quarter, quarter)


def mix_table():
    row = lax.broadcasted_iota(jnp.int32, (256, 256), 0)
    column = lax.broadcasted_iota(jnp.int32, (256, 256), 1)
    same = ((row >> 2) & 1) * 16 + ((row >> 3) & 15) == (column & 31)
    power = ((row & 3) * ((column >> 5) & 3) + (row >> 7) - (column >> 7)) & 3
    value = jnp.where(power & 1 == 1, 0.0, jnp.where(power == 0, 1.0, -1.0))
    return jnp.where(same, value, 0.0).astype(bf16)


def middle_kernel(place, arrived, *refs):
    echoes, given, out, sent = refs[:8], refs[8:10], refs[10], refs[11:19]
    held, resid = refs[19:]
    for step in range(8):
        held[(place[0] + 8 - step) & 7] = echoes[step][...]
    parts = []
    for k in range(3):
        rows = []
        for odd in range(2):
            pieces = [held[2 * t1 + odd, k * 64 : (k + 1) * 64, :] for t1 in range(4)]
            rows += swap_groups(pieces, 32)
        parts.append(jnp.concatenate(rows, 0))
    long = [given[0].at[pl.ds(256 * k, 256)] for k in range(4)]
    twist, mix = given[1], mix_table()
    both_twists, odd_twist = sent_twists(twist)
    pairs = [
        tuple(arrived[pl.ds(2 * p + c, 256, stride=4), :] for c in range(2)) for p in range(2)
    ]
    even, odd = [
        (cos_re - sin_im, sin_re + cos_im)
        for cos_re, cos_im, sin_re, sin_im in half_sums(pairs, long)
    ]
    odd = turned(odd, odd_twist)
    value = [jnp.concatenate([a + b, a - b], 0) for a, b in zip(even, odd)]
    both = jnp.concatenate(turned(value, both_twists), 1)
    high, rest = split(both)
    field = dot(high, mix) + dot(rest, mix)
    left = []
    for k in range(2):
        value = parts[2] * (parts[k] - field[:, k * 128 : (k + 1) * 128])
        left.append(value)
        for odd in range(2):
            pieces = [value[odd * 256 + q * 64 : odd * 256 + (q + 1) * 64] for q in range(4)]
            for t1, piece in enumerate(swap_groups(pieces, 32)):
                resid[2 * t1 + odd, k * 64 : (k + 1) * 64, :] = piece
    for step in range(8):
        sent[step][...] = resid[(place[0] + step) & 7]
    mixed = sum(
        lax.dot_general(half, mix, nt_form, preferred_element_type=f32)
        for half in split(jnp.concatenate(left, 1))
    )
    value = turned_back((mixed[:, :128], mixed[:, 128:]), both_twists)
    even = [part[:256] + part[256:] for part in value]
    odd = turned_back([part[:256] - part[256:] for part in value], odd_twist)
    for p, sums in enumerate(half_sums([even, odd], long)):
        cos_re, cos_im, sin_re, sin_im = sums
        out[pl.ds(2 * p, 256, stride=4), :] = cos_re + sin_im
        out[pl.ds(2 * p + 1, 256, stride=4), :] = cos_im - sin_re


def call(kernel, outs, *operands, near=0, apart=0, far=False, scratch=(), place=None, flops=0):
    single = not isinstance(outs, list)
    outs = [outs] if single else outs
    outs = [jax.ShapeDtypeStruct(o, f32) for o in outs]
    moved = sum(math.prod(o.shape) * o.dtype.itemsize for o in [*outs, *operands])
    spec = pl.BlockSpec(memory_space=pltpu.VMEM)
    in_specs = [spec] * (len(operands) - apart) + [pl.BlockSpec(memory_space=pl.ANY)] * apart
    operands = [
        pltpu.with_memory_space_constraint(o, pltpu.VMEM) if k < near else o
        for k, o in enumerate(operands)
    ]
    if place is not None:
        operands = [place, *operands]
        in_specs = [pl.BlockSpec(memory_space=pltpu.SMEM), *in_specs]
    out = pl.pallas_call(
        kernel,
        out_shape=outs if far else [pltpu.VMEM(o.shape, o.dtype) for o in outs],
        in_specs=in_specs,
        out_specs=[spec] * len(outs),
        scratch_shapes=[pltpu.VMEM(s, f32) if isinstance(s, tuple) else s for s in scratch],
        compiler_params=params,
        cost_estimate=pl.CostEstimate(flops=flops, bytes_accessed=moved, transcendentals=0),
    )(*operands)
    return out[0] if single else out


def exchange(value, axes):
    return lax.all_to_all(value, axes, split_axis=0, concat_axis=0, tiled=True)


def along_tx(pieces):
    moved = [pieces[0]]
    for step in range(1, 8):
        moved.append(lax.ppermute(pieces[step], "tx", [(i, (i + step) % 8) for i in range(8)]))
    return moved


def wave_numbers(indices, total):
    signed = jnp.where(indices < total // 2, indices, indices - total)
    return 2.0 * jnp.pi / total * signed.astype(f32)


def turns(wavenumber, tx, z, y):
    low = jnp.arange(8, dtype=jnp.int32) % 4
    sent = wave_numbers(tx * 256 + z * 16 + y * 4 + low, 2048)
    heard = wave_numbers(jnp.arange(2048, dtype=jnp.int32).reshape(16, 1, 1, 128), 2048)
    waves = jnp.repeat(wavenumber.reshape(4, 2), 4, axis=1)
    squared = waves * waves
    first = jnp.sqrt(jnp.maximum(squared - (sent * sent)[None, :], 0.0) + root_floor)
    second = jnp.sqrt(
        jnp.maximum(squared[None, :, :, None] - heard * heard, 0.0) + root_floor
    )
    phase = depth_step * (first[None, :, :, None] + second)
    return jnp.stack([jnp.cos(phase), jnp.sin(phase)])


def per_device(spectrum, measured, wavenumber, send_weight, hear_weight, aperture):
    table = tables()
    tx, z, y = lax.axis_index("tx"), lax.axis_index("rx"), lax.axis_index("freq")

    sent = call(send_kernel, (32, 2, 2, 8, 128), spectrum)
    arrived = exchange(sent.reshape(64, 16, 128), ("rx", "freq"))

    turn = turns(wavenumber, tx, z, y)
    place = tx.astype(jnp.int32).reshape(1)
    packed = call(
        pack_kernel,
        [(192, 128)] * 8,
        measured,
        send_weight.reshape(2, 128),
        hear_weight.reshape(1, 128),
        aperture,
        scratch=[(8, 192, 128)],
        place=place,
    )
    echoes = along_tx(packed)
    early = echoes[:early_echoes]
    pairs = call(
        pair_kernel,
        (1024, 128),
        arrived.reshape(16, 4, 2, 8, 128),
        turn,
        table["twist_heard"],
        *table["lanes"],
        *early,
        near=5,
        apart=len(early),
        flops=10**9,
    )
    columns = exchange(pairs.reshape(512, 2, 128), ("tx", "rx", "freq")).reshape(1024, 128)
    given = [np.concatenate(table["long"], 0), table["twist_sent"]]
    back, *resid = call(
        middle_kernel,
        [(1024, 128)] + [(128, 128)] * 8,
        columns,
        *echoes,
        *given,
        near=11,
        scratch=[(8, 192, 128), (8, 128, 128)],
        place=place,
        flops=3 * 10**9,
    )
    rows = exchange(back.reshape(512, 2, 128), ("tx", "rx", "freq")).reshape(1024, 128)
    pieces = along_tx(resid)
    residual = call(
        unpack_kernel,
        (2, 2, 256, 128),
        *pieces,
        near=8,
        far=True,
        scratch=[(8, 128, 128)],
        place=place,
    )
    early = pieces[:early_pieces]
    gradient = call(
        gradient_kernel,
        (16, 4, 2, 8, 128),
        rows,
        turn,
        table["twist_heard"],
        *table["lanes"],
        *early,
        near=5,
        apart=len(early),
        scratch=[(4, 16, 2, 8, 128)],
        flops=10**9,
    )
    gathered = exchange(gradient.reshape(64, 16, 128), ("rx", "freq"))
    updated = call(
        update_kernel,
        (2, 2, 256, 128),
        gathered.reshape(32, 2, 2, 8, 128),
        spectrum,
        near=2,
        far=True,
    )
    return updated, residual


def solution(mesh):
    placed = (
        P(None, "freq", "tx", "rx"),
        P(None, "freq", "tx", "rx"),
        P(),
        P("tx"),
        P("rx"),
        P("tx", "rx"),
    )
    return jax.shard_map(
        per_device,
        mesh=mesh,
        in_specs=placed,
        out_specs=(P(None, "freq", "tx", "rx"), P(None, "freq", "tx", "rx")),
        check_vma=False,
    )
```
